1024 devices in a mesh: dp: 64 (over z_hi, y, core), tensor: 16 (over z_lo, x).
Axes of the slice: x: 8, y: 8, z: 8 (z_hi: 4, z_lo: 2; z = z_hi * 2 + z_lo), core: 2. Of those that a mesh axis runs over, the one named last changes fastest.
Arguments:
- tokens: bfloat16 [8192, 4096], P(('dp', 'tensor')), may hold values from -6 to 6
- grad_out: bfloat16 [8192, 4096], P(('dp', 'tensor')), may hold values from -6 to 6
- gate_tiles: bfloat16 [16, 16, 128, 128], P('tensor'), may hold values from -0.25 to 0.25
- up_tiles: bfloat16 [16, 16, 128, 128], P('tensor'), may hold values from -0.25 to 0.25
- down_tiles: bfloat16 [16, 16, 128, 128], P('tensor'), may hold values from -0.1875 to 0.1875
- gate_index: int32 [16, 16], P('tensor'), may hold values from -1 to 127, as said below
- up_index: int32 [16, 16], P('tensor'), may hold values from -1 to 127, as said below
- down_index: int32 [16, 16], P('tensor'), may hold values from -1 to 127, as said below
Outputs:
- input_grad: bfloat16 [8192, 4096], P(('dp', 'tensor'))
- tile_grads: float32 [16, 2048, 384], P('tensor', 'dp')
The draws below stay inside these ranges and needn't reach their ends.
Inputs may be any that keep to these rules, and one draw needn't show every extreme that they name: `gate_index`: in each index array every row lists distinct positions in its first slots and -1 in the rest; each row uses at least 5 slots and some row uses all 16. `up_index`: as for gate_index, drawn apart. `down_index`: as for gate_index, drawn apart.
All inputs are finite; a program needn't handle non-finite values.
Results may differ from the reference program's by a relative error of at most 0.017.
Values may be sent and summed in bfloat16 or wider, within the bound.
No kernel may reach another device: no remote copies, remote signals or barrier semaphores. Data moves between devices by JAX's collectives and lax.ppermute only.
A program may use at most 32 MiB of HBM per device.

```python
import jax
import jax.numpy as jnp
from jax import lax

D = 4096
FF = 8192
TILE = 128
DB = 32
HB_DEV = 4
GRID = 128
CAP = 16
ROWS = 128
TOKENS = 8192
N_DP = 64
N_TENSOR = 16


def tile_slots(key, salt):
    key = jax.random.fold_in(key, salt)
    k_count, k_busy, k_perm = jax.random.split(key, 3)
    counts = jax.random.randint(k_count, (N_TENSOR,), CAP // 3, CAP + 1)
    busiest = jax.random.randint(k_busy, (), 0, N_TENSOR)
    counts = jnp.where(jnp.arange(N_TENSOR) == busiest, CAP, counts)
    keys = jax.random.split(k_perm, N_TENSOR)

    def one_order(one_key):
        return jax.random.permutation(one_key, GRID)
    order = jax.vmap(one_order)(keys)[:, :CAP]
    slots = jnp.arange(CAP)
    return jnp.where(slots[None, :] < counts[:, None], order, -1).astype(jnp.int32)


def draw_gate_index(key, part):
    return tile_slots(key, 11)


def draw_up_index(key, part):
    return tile_slots(key, 23)


def draw_down_index(key, part):
    return tile_slots(key, 37)


def block_levels(rng, dims, cuts, smallest, top_value):
    factor_of = 1.0
    for axis_at, parts in cuts:
        draws = jax.random.uniform(jax.random.fold_in(jax.random.fold_in(rng, 6), axis_at), (parts,), jnp.float32, smallest / len(cuts), top_value / len(cuts))
        factor_of = factor_of * jnp.repeat(jnp.exp(draws), dims[axis_at] // parts).reshape((-1,) + (1,) * (len(dims) - 1 - axis_at))
    return factor_of


def gaussian(stream_key, shape, scale, limit, cuts=(), kind=jnp.bfloat16):
    loudness = block_levels(stream_key, shape, cuts, -0.22, 0.18) if cuts else 1.0
    array = jax.random.normal(stream_key, shape, jnp.float32) * scale * loudness
    return jnp.minimum(jnp.maximum(array, -limit), limit).astype(kind)


def setup_inputs(seed: int = 0) -> dict:
    seeds = jax.random.split(jax.random.key(seed), 9)
    tokens = gaussian(seeds[0], (TOKENS, D), 1.0, 6.0, ((0, 1024),))
    grad_out = gaussian(seeds[1], (TOKENS, D), 1.0, 6.0, ((0, 1024),))
    gate_tiles = gaussian(seeds[2], (N_TENSOR, CAP, TILE, TILE), (D // 8) ** -0.5, 0.25, ((0, 16),))
    up_tiles = gaussian(seeds[3], (N_TENSOR, CAP, TILE, TILE), (D // 8) ** -0.5, 0.25, ((0, 16),))
    down_tiles = gaussian(seeds[4], (N_TENSOR, CAP, TILE, TILE), (FF // 8) ** -0.5, 0.1875, ((0, 16),))
    gate_index = draw_gate_index(jax.random.fold_in(seeds[8], 71), 0)
    up_index = draw_up_index(jax.random.fold_in(seeds[8], 71), 0)
    down_index = draw_down_index(jax.random.fold_in(seeds[8], 71), 0)
    return {"tokens": tokens, "grad_out": grad_out, "gate_tiles": gate_tiles, "up_tiles": up_tiles, "down_tiles": down_tiles, "gate_index": gate_index, "up_index": up_index, "down_index": down_index}


def split_index(index, width):
    live = index >= 0
    safe = jnp.where(live, index, 0).astype(jnp.int32)
    return safe // width, safe % width, live


def onehot(picks, live, count):
    table = (picks[:, None] == jnp.arange(count, dtype=jnp.int32)[None, :]) & live[:, None]
    return table.astype(jnp.float32)


def spread(slot_vals, table):
    return jnp.einsum("rsn,sc->rcn", slot_vals, table, precision=lax.Precision.HIGHEST)


def product(form, left, right):
    return jnp.einsum(form, left.astype(jnp.float32), right.astype(jnp.float32), precision=lax.Precision.HIGHEST)


def shard_pass(whole_rows, whole_grads, gate_w, up_w, down_w, g_index, u_index, d_index):
    rows = whole_rows.shape[0]
    x_blocks = whole_rows.reshape(rows, DB, TILE)
    dy_blocks = whole_grads.reshape(rows, DB, TILE)
    g_row, g_col, g_live = split_index(g_index, HB_DEV)
    u_row, u_col, u_live = split_index(u_index, HB_DEV)
    d_hid, d_col, d_live = split_index(d_index, DB)
    g_sel = jnp.take(x_blocks, g_row, axis=1)
    u_sel = jnp.take(x_blocks, u_row, axis=1)
    gate = spread(product("rsk,skn->rsn", g_sel, gate_w), onehot(g_col, g_live, HB_DEV))
    up = spread(product("rsk,skn->rsn", u_sel, up_w), onehot(u_col, u_live, HB_DEV))
    sig = jax.nn.sigmoid(gate)
    act = gate * sig
    hidden = (act * up).astype(jnp.bfloat16)
    dy_sel = jnp.take(dy_blocks, d_col, axis=1)
    dhidden = spread(product("rsn,skn->rsk", dy_sel, down_w), onehot(d_hid, d_live, HB_DEV))
    h_sel = jnp.take(hidden, d_hid, axis=1)
    down_grad = product("rsk,rsn->skn", h_sel, dy_sel) * d_live[:, None, None].astype(jnp.float32)
    dgate = (dhidden * up * sig * (1.0 + gate * (1.0 - sig))).astype(jnp.bfloat16)
    dup = (dhidden * act).astype(jnp.bfloat16)
    dg_sel = jnp.take(dgate, g_col, axis=1)
    du_sel = jnp.take(dup, u_col, axis=1)
    gate_grad = product("rsk,rsn->skn", g_sel, dg_sel) * g_live[:, None, None].astype(jnp.float32)
    up_grad = product("rsk,rsn->skn", u_sel, du_sel) * u_live[:, None, None].astype(jnp.float32)
    part = spread(product("rsn,skn->rsk", dg_sel, gate_w), onehot(g_row, g_live, DB))
    part = part + spread(product("rsn,skn->rsk", du_sel, up_w), onehot(u_row, u_live, DB))
    grads = jnp.concatenate([gate_grad, up_grad, down_grad], axis=2)
    return part.reshape(rows, DB * TILE), grads


def reference(tokens, grad_out, gate_tiles, up_tiles, down_tiles, gate_index, up_index, down_index):
    x_groups = tokens.reshape(N_DP, ROWS, D)
    dy_groups = grad_out.reshape(N_DP, ROWS, D)
    shards = (gate_tiles, up_tiles, down_tiles, gate_index, up_index, down_index)

    def one_group(total, pair):
        whole_rows, whole_grads = pair

        def one_shard(accum, shard):
            part, grads = shard_pass(whole_rows, whole_grads, *shard)
            rounded = lax.optimization_barrier(part.astype(jnp.bfloat16))
            return accum + rounded.astype(jnp.float32), grads

        summed, grads = lax.scan(one_shard, jnp.zeros((ROWS, D), jnp.float32), shards)
        return total + grads, summed.astype(jnp.bfloat16)

    start = jnp.zeros((N_TENSOR, CAP, TILE, 3 * TILE), jnp.float32)
    total, input_grad = lax.scan(one_group, start, (x_groups, dy_groups))
    return input_grad.reshape(TOKENS, D), total.reshape(N_TENSOR, CAP * TILE, 3 * TILE)
```

```python
import jax
import jax.numpy as jnp
from jax import lax
from jax.experimental import pallas as pl
from jax.experimental.pallas import tpu as pltpu
from jax.sharding import Mesh, PartitionSpec as P

TILE = 128
DP = ("zh", "y", "c")
TEN = ("zl", "x")
F32 = jnp.float32
BF16 = jnp.bfloat16


def lanes(ref, tile_at):
    return ref[:, pl.ds(pl.multiple_of(tile_at * TILE, TILE), TILE)]


def dot(left, right, on):
    return lax.dot_general(left, right, ((on[:1], on[1:]), ((), ())), preferred_element_type=F32)


def front(
    g_idx, u_idx, d_idx, core, xa, gw, uw, dw, mine, theirs, dgate, dup, gate, up, dhid, hid
):
    slots = gw.shape[0]
    blocks = xa.shape[1] // TILE // 2
    for acc in (gate, up, dhid):
        acc[...] = jnp.zeros_like(acc)
    for s in range(slots):
        for idx, w, acc in ((g_idx, gw, gate), (u_idx, uw, up)):
            v = idx[0, s]
            safe = jnp.maximum(v, 0)
            col = safe & 3
            val = dot(lanes(xa, safe >> 2), w[s], (1, 0))
            acc[col] += jnp.where(v >= 0, val, 0.0)
        v = d_idx[0, s]
        safe = jnp.maximum(v, 0)
        val = dot(lanes(xa, blocks + safe % blocks), dw[s], (1, 1))
        row = safe // blocks
        dhid[row] += jnp.where(v >= 0, val, 0.0)
    for b in range(gate.shape[0]):
        g, u, dh = gate[b], up[b], dhid[b]
        sig = jax.nn.sigmoid(g)
        act = g * sig
        hid[b] = (act * u).astype(BF16)
        dgate[b] = (dh * u * sig * (1.0 + g * (1.0 - sig))).astype(BF16)
        dup[b] = (dh * act).astype(BF16)
    first = core[0] == 0
    for s in range(slots):
        outs = []
        for idx, grad in ((g_idx, dgate), (u_idx, dup)):
            v = idx[0, s]
            safe = jnp.maximum(v, 0)
            val = dot(lanes(xa, safe >> 2), grad[safe & 3], (0, 0))
            outs.append(jnp.where(v >= 0, val, 0.0))
        v = d_idx[0, s]
        safe = jnp.maximum(v, 0)
        val = dot(hid[safe // blocks], lanes(xa, blocks + safe % blocks), (0, 0))
        outs.append(jnp.where(v >= 0, val, 0.0))
        for k, val in enumerate(outs):
            for half in range(2):
                even = val[64 * half : 64 * half + 32]
                odd = val[64 * half + 32 : 64 * half + 64]
                at = (2 * s + half, slice(None), slice(k * TILE, (k + 1) * TILE))
                mine[at] = jnp.where(first, even, odd)
                theirs[at] = jnp.where(first, odd, even).astype(BF16)


def back(g_idx, u_idx, dgate, dup, gw, uw, part, acc):
    acc[...] = jnp.zeros_like(acc)
    for s in range(gw.shape[0]):
        for idx, w, grad in ((g_idx, gw, dgate), (u_idx, uw, dup)):
            v = idx[0, s]
            safe = jnp.maximum(v, 0)
            val = dot(grad[safe & 3], w[s], (1, 1))
            row = safe >> 2
            acc[row] += jnp.where(v >= 0, val, 0.0)
    for b in range(acc.shape[0]):
        part[:, b * TILE : (b + 1) * TILE] = acc[b].astype(BF16)


SMEM = pl.BlockSpec(memory_space=pltpu.SMEM)
VMEM = pl.BlockSpec(memory_space=pltpu.VMEM)


def per_device(
    tokens, grad_out, gate_tiles, up_tiles, down_tiles, gate_index, up_index, down_index
):
    here, width = tokens.shape
    ten, dp = lax.axis_size(TEN), lax.axis_size(DP)
    rows, slots = here * ten, gate_tiles.shape[1]
    blocks = width // TILE
    hidden = 4
    gw, uw, dw = gate_tiles[0], up_tiles[0], down_tiles[0]
    core = lax.axis_index("c").astype(jnp.int32).reshape(1)
    with jax.named_scope("gather"):
        both = jnp.concatenate([tokens, grad_out], axis=1)
        send = jnp.broadcast_to(both[None], (ten, here, 2 * width))
        xa = lax.all_to_all(send, TEN, 0, 0, tiled=True).reshape(rows, 2 * width)
    half = dp // 2
    mine, theirs, dgate, dup = pl.pallas_call(
        front,
        out_shape=(
            jax.ShapeDtypeStruct((half, 32, 3 * TILE), F32),
            jax.ShapeDtypeStruct((half, 32, 3 * TILE), BF16),
            jax.ShapeDtypeStruct((hidden, rows, TILE), BF16),
            jax.ShapeDtypeStruct((hidden, rows, TILE), BF16),
        ),
        in_specs=[SMEM] * 4 + [VMEM] * 4,
        out_specs=(VMEM,) * 4,
        scratch_shapes=[pltpu.VMEM((hidden, rows, TILE), F32)] * 3
        + [pltpu.VMEM((hidden, rows, TILE), BF16)],
        compiler_params=pltpu.CompilerParams(vmem_limit_bytes=24 << 20),
        cost_estimate=pl.CostEstimate(
            flops=96 * 2 * TILE**3, bytes_accessed=8 << 20, transcendentals=1 << 16
        ),
        name="front",
    )(gate_index, up_index, down_index, core, xa, gw, uw, dw)
    with jax.named_scope("cores"):
        got = lax.ppermute(theirs, "c", [(0, 1), (1, 0)])
    part = pl.pallas_call(
        back,
        out_shape=jax.ShapeDtypeStruct((rows, width), BF16),
        in_specs=[SMEM] * 2 + [VMEM] * 4,
        out_specs=VMEM,
        scratch_shapes=[pltpu.VMEM((blocks, rows, TILE), F32)],
        compiler_params=pltpu.CompilerParams(vmem_limit_bytes=16 << 20),
        cost_estimate=pl.CostEstimate(
            flops=32 * 2 * TILE**3, bytes_accessed=3 << 20, transcendentals=0
        ),
        name="back",
    )(gate_index, up_index, dgate, dup, gw, uw)
    with jax.named_scope("partials"):
        parts = lax.all_to_all(part.reshape(ten, here, width), TEN, 0, 0, tiled=True)
        input_sum = jnp.sum(parts.astype(F32), axis=0).astype(BF16)
    with jax.named_scope("tile_sums"):
        pair = (mine + got.astype(F32)).astype(BF16)
        grads = lax.all_to_all(pair, ("zh", "y"), 0, 0, tiled=True)
        sums = jnp.sum(grads.astype(F32), axis=0)
    return (input_sum, sums[None])


def solution(mesh):
    fine = Mesh(mesh.devices.reshape(4, 8, 2, 2, 8), DP + TEN)
    both = P(DP + TEN, None)
    return jax.shard_map(
        per_device,
        mesh=fine,
        in_specs=(both, both)
        + (P(TEN, None, None, None),) * 3
        + (P(TEN, None),) * 3,
        out_specs=(both, P(TEN, DP, None)),
        check_vma=False,
    )
```

```python
import jax
import jax.numpy as jnp
from jax import lax
from jax.experimental import pallas as pl
from jax.experimental.pallas import tpu as pltpu
from jax.sharding import Mesh, PartitionSpec as P

TILE = 128
DP = ("zh", "y", "c")
TEN = ("zl", "x")
F32 = jnp.float32
BF16 = jnp.bfloat16


def lanes(ref, tile_at):
    return ref[:, pl.ds(pl.multiple_of(tile_at * TILE, TILE), TILE)]


def dot(left, right, on):
    return lax.dot_general(left, right, ((on[:1], on[1:]), ((), ())), preferred_element_type=F32)


def slot_list(core, own, far, own_w, far_w):
    slots = own_w[0].shape[0]
    half = slots // 2
    for j in range(slots):
        at = [core * half + j % half, (1 - core) * half + j % half][j // half]
        k = j % half
        yield 1, at, [far[0, n * slots + at] for n in range(3)], [far_w[j // half].at[n, k] for n in range(3)]
    for s in range(slots):
        yield 0, s, [i[0, s] for i in own], [w.at[s] for w in own_w]


def front(
    g_idx, u_idx, d_idx, far, core, xa, gw, uw, dw, ra, rb,
    own_mine, own_theirs, far_mine, far_theirs, dgate, dup, gate, up, dhid, hid,
):
    blocks = xa.shape[1] // TILE // 2
    hidden = gate.shape[0] // 2
    slots = list(slot_list(core[0], (g_idx, u_idx, d_idx), far, (gw, uw, dw), (ra, rb)))
    for acc in (gate, up, dhid):
        acc[...] = jnp.zeros_like(acc)
    for side, _, (gv, uv, dv), (g_t, u_t, d_t) in slots:
        for v, w, acc in ((gv, g_t, gate), (uv, u_t, up)):
            safe = jnp.maximum(v, 0)
            val = dot(lanes(xa, safe >> 2), w[...], (1, 0))
            acc[side * hidden + (safe & 3)] += jnp.where(v >= 0, val, 0.0)
        safe = jnp.maximum(dv, 0)
        val = dot(lanes(xa, blocks + (safe & 31)), d_t[...], (1, 1))
        dhid[side * hidden + (safe >> 5)] += jnp.where(dv >= 0, val, 0.0)
    for b in range(gate.shape[0]):
        g, u, dh = gate[b], up[b], dhid[b]
        sig = jax.nn.sigmoid(g)
        act = g * sig
        hid[b] = (act * u).astype(BF16)
        dgate[b] = (dh * u * sig * (1.0 + g * (1.0 - sig))).astype(BF16)
        dup[b] = (dh * act).astype(BF16)
    first = core[0] == 0
    for side, slot, (gv, uv, dv), _ in slots:
        mine, theirs = ((own_mine, own_theirs), (far_mine, far_theirs))[side]
        outs = []
        for v, grad in ((gv, dgate), (uv, dup)):
            safe = jnp.maximum(v, 0)
            val = dot(lanes(xa, safe >> 2), grad[side * hidden + (safe & 3)], (0, 0))
            outs.append(jnp.where(v >= 0, val, 0.0))
        safe = jnp.maximum(dv, 0)
        val = dot(hid[side * hidden + (safe >> 5)], lanes(xa, blocks + (safe & 31)), (0, 0))
        outs.append(jnp.where(dv >= 0, val, 0.0))
        for k, val in enumerate(outs):
            for half in range(2):
                even = val[64 * half : 64 * half + 32]
                odd = val[64 * half + 32 : 64 * half + 64]
                at = (2 * slot + half, slice(None), slice(k * TILE, (k + 1) * TILE))
                mine[at] = jnp.where(first, even, odd)
                theirs[at] = jnp.where(first, odd, even).astype(BF16)


def back(g_idx, u_idx, far, core, dgate, dup, gw, uw, ra, rb, part, acc):
    hidden = dgate.shape[0] // 2
    acc[...] = jnp.zeros_like(acc)
    for side, _, vs, ws in slot_list(core[0], (g_idx, u_idx, u_idx), far, (gw, uw, uw), (ra, rb)):
        for v, w, grad in zip(vs[:2], ws[:2], (dgate, dup)):
            safe = jnp.maximum(v, 0)
            val = dot(grad[side * hidden + (safe & 3)], w[...], (1, 1))
            acc[safe >> 2] += jnp.where(v >= 0, val, 0.0)
    for b in range(acc.shape[0]):
        part[:, b * TILE : (b + 1) * TILE] = acc[b].astype(BF16)


SMEM = pl.BlockSpec(memory_space=pltpu.SMEM)
VMEM = pl.BlockSpec(memory_space=pltpu.VMEM)
SWAP = [(0, 1), (1, 0)]


def per_device(
    tokens, grad_out, gate_tiles, up_tiles, down_tiles, gate_index, up_index, down_index
):
    here, width = tokens.shape
    line = lax.axis_size("x")
    rows, slots = here * line, gate_tiles.shape[1]
    blocks, hidden = width // TILE, 8
    pairs = lax.axis_size(DP) // 2
    gw, uw, dw = gate_tiles[0], up_tiles[0], down_tiles[0]
    at_core = lax.axis_index("c").astype(jnp.int32)
    core = at_core.reshape(1)
    with jax.named_scope("gather"):
        both = jnp.concatenate([tokens, grad_out], axis=1)
        send = jnp.broadcast_to(both[None], (line, here, 2 * width))
        xa = lax.all_to_all(send, "x", 0, 0, tiled=True).reshape(rows, 2 * width)
    with jax.named_scope("weights"):
        part_of = lambda w: lax.dynamic_slice_in_dim(w, at_core * (slots // 2), slots // 2)
        far = lax.ppermute(
            jnp.concatenate([gate_index, up_index, down_index], axis=1), "zl", SWAP
        )
        ra = lax.ppermute(jnp.stack([part_of(w) for w in (gw, uw, dw)]), "zl", SWAP)
        rb = lax.ppermute(ra, "c", SWAP)
    own_mine, own_theirs, far_mine, far_theirs, dgate, dup = pl.pallas_call(
        front,
        out_shape=(
            jax.ShapeDtypeStruct((pairs, 32, 3 * TILE), F32),
            jax.ShapeDtypeStruct((pairs, 32, 3 * TILE), BF16),
        )
        * 2
        + (jax.ShapeDtypeStruct((hidden, rows, TILE), BF16),) * 2,
        in_specs=[SMEM] * 5 + [VMEM] * 6,
        out_specs=(VMEM,) * 6,
        scratch_shapes=[pltpu.VMEM((hidden, rows, TILE), F32)] * 3
        + [pltpu.VMEM((hidden, rows, TILE), BF16)],
        compiler_params=pltpu.CompilerParams(vmem_limit_bytes=24 << 20),
        cost_estimate=pl.CostEstimate(
            flops=96 * 2 * TILE**3, bytes_accessed=8 << 20, transcendentals=1 << 16
        ),
        name="front",
    )(gate_index, up_index, down_index, far, core, xa, gw, uw, dw, ra, rb)
    with jax.named_scope("cores"):
        far_got = lax.ppermute(far_theirs, "c", SWAP)
        own_got = lax.ppermute(own_theirs, "c", SWAP)
    part = pl.pallas_call(
        back,
        out_shape=jax.ShapeDtypeStruct((rows, width), BF16),
        in_specs=[SMEM] * 4 + [VMEM] * 6,
        out_specs=VMEM,
        scratch_shapes=[pltpu.VMEM((blocks, rows, TILE), F32)],
        compiler_params=pltpu.CompilerParams(vmem_limit_bytes=16 << 20),
        cost_estimate=pl.CostEstimate(
            flops=32 * 2 * TILE**3, bytes_accessed=3 << 20, transcendentals=0
        ),
        name="back",
    )(gate_index, up_index, far, core, dgate, dup, gw, uw, ra, rb)
    with jax.named_scope("layers"):
        near = lax.ppermute((far_mine + far_got.astype(F32)).astype(BF16), "zl", SWAP)
    with jax.named_scope("partials"):
        parts = lax.all_to_all(part.reshape(line, here, width), "x", 0, 0, tiled=True)
        input_sum = jnp.sum(parts.astype(F32), axis=0).astype(BF16)
    with jax.named_scope("tile_sums"):
        quad = (own_mine + own_got.astype(F32) + near.astype(F32)).astype(BF16)
        grads = lax.all_to_all(quad, ("zh", "y"), 0, 0, tiled=True)
        sums = jnp.sum(grads.astype(F32), axis=0)
    return (input_sum, sums[None])


def solution(mesh):
    fine = Mesh(mesh.devices.reshape(4, 8, 2, 2, 8), DP + TEN)
    both = P(DP + TEN, None)
    return jax.shard_map(
        per_device,
        mesh=fine,
        in_specs=(both, both)
        + (P(TEN, None, None, None),) * 3
        + (P(TEN, None),) * 3,
        out_specs=(both, P(TEN, DP, None)),
        check_vma=False,
    )
```

```python
import jax
import jax.numpy as jnp
from jax import lax
from jax.experimental import pallas as pl
from jax.experimental.pallas import tpu as pltpu
from jax.sharding import Mesh, PartitionSpec as P

TILE = 128
DP = ("zh", "y", "c")
TEN = ("zl", "x")
F32 = jnp.float32
BF16 = jnp.bfloat16


def lanes(ref, tile_at):
    return ref[:, pl.ds(pl.multiple_of(tile_at * TILE, TILE), TILE)]


def dot(left, right, on):
    return lax.dot_general(left, right, ((on[:1], on[1:]), ((), ())), preferred_element_type=F32)


def fetch(halves, held, sems):
    copies = [pltpu.make_async_copy(r, held.at[h], sems.at[h]) for h, r in enumerate(halves)]
    for copy in copies:
        copy.start()
    return copies


def slot_list(core, own, far, own_w, held, copies):
    slots = own_w[0].shape[0]
    half = slots // 2
    for s in range(slots):
        yield 0, [i[0, s] for i in own], [w.at[s] for w in own_w]
    for j in range(slots):
        h, k = divmod(j, half)
        if k == 0:
            copies[h].wait()
        at = (core if h == 0 else 1 - core) * half + k
        yield 1, [far[0, n * slots + at] for n in range(3)], [held.at[h, n, k] for n in range(3)]


def forward(
    g_idx, u_idx, d_idx, far, core, xa, gw, uw, dw, ra, rb, dgate, dup, hid, held, sems, gate, up, dhid
):
    copies = fetch((ra, rb), held, sems)
    blocks = xa.shape[1] // TILE // 2
    hidden = gate.shape[0] // 2
    for acc in (gate, up, dhid):
        acc[...] = jnp.zeros_like(acc)
    slots = slot_list(core[0], (g_idx, u_idx, d_idx), far, (gw, uw, dw), held, copies)
    for side, (gv, uv, dv), (g_t, u_t, d_t) in slots:
        for v, w, acc in ((gv, g_t, gate), (uv, u_t, up)):
            safe = jnp.maximum(v, 0)
            val = dot(lanes(xa, safe >> 2), w[...], (1, 0))
            acc[side * hidden + (safe & 3)] += jnp.where(v >= 0, val, 0.0)
        safe = jnp.maximum(dv, 0)
        val = dot(lanes(xa, blocks + (safe & 31)), d_t[...], (1, 1))
        dhid[side * hidden + (safe >> 5)] += jnp.where(dv >= 0, val, 0.0)
    for b in range(gate.shape[0]):
        g, u, dh = gate[b], up[b], dhid[b]
        sig = jax.nn.sigmoid(g)
        act = g * sig
        hid[b] = (act * u).astype(BF16)
        dgate[b] = (dh * u * sig * (1.0 + g * (1.0 - sig))).astype(BF16)
        dup[b] = (dh * act).astype(BF16)


def back(g_idx, u_idx, far, core, dgate, dup, gw, uw, ra, rb, part, held, sems, acc):
    copies = fetch((ra, rb), held, sems)
    hidden = dgate.shape[0] // 2
    acc[...] = jnp.zeros_like(acc)
    slots = slot_list(core[0], (g_idx, u_idx, u_idx), far, (gw, uw, uw), held, copies)
    for side, vs, ws in slots:
        for v, w, grad in zip(vs[:2], ws[:2], (dgate, dup)):
            safe = jnp.maximum(v, 0)
            val = dot(grad[side * hidden + (safe & 3)], w[...], (1, 1))
            acc[safe >> 2] += jnp.where(v >= 0, val, 0.0)
    for b in range(acc.shape[0]):
        part[:, b * TILE : (b + 1) * TILE] = acc[b]


def tile_terms(
    g_idx, u_idx, d_idx, far, core, xa, dgate, dup, hid, own_mine, own_theirs, far_mine, far_theirs
):
    blocks = xa.shape[1] // TILE // 2
    hidden = dgate.shape[0] // 2
    first = core[0] == 0
    sets = (
        (1, lambda n, s: far[0, n * CAP + s], far_mine, far_theirs),
        (0, lambda n, s: (g_idx, u_idx, d_idx)[n][0, s], own_mine, own_theirs),
    )
    for side, index, mine, theirs in sets:
        for slot in range(CAP):
            outs = []
            for n, grad in ((0, dgate), (1, dup)):
                v = index(n, slot)
                safe = jnp.maximum(v, 0)
                val = dot(lanes(xa, safe >> 2), grad[side * hidden + (safe & 3)], (0, 0))
                outs.append(jnp.where(v >= 0, val, 0.0))
            v = index(2, slot)
            safe = jnp.maximum(v, 0)
            val = dot(hid[side * hidden + (safe >> 5)], lanes(xa, blocks + (safe & 31)), (0, 0))
            outs.append(jnp.where(v >= 0, val, 0.0))
            for k, val in enumerate(outs):
                for half in range(2):
                    even = val[64 * half : 64 * half + 32]
                    odd = val[64 * half + 32 : 64 * half + 64]
                    at = (2 * slot + half, slice(None), slice(k * TILE, (k + 1) * TILE))
                    mine[at] = jnp.where(first, even, odd).astype(BF16)
                    theirs[at] = jnp.where(first, odd, even).astype(BF16)


def beside():
    pairs = []
    for zh in range(4):
        for c in range(2):
            for zl in range(2):
                to = (zh if c == 0 else (zh + (1 if zl else -1)) % 4, c, 1 - zl)
                pairs.append(((zh * 2 + c) * 2 + zl, (to[0] * 2 + to[1]) * 2 + to[2]))
    return pairs


CAP = 16

SMEM = pl.BlockSpec(memory_space=pltpu.SMEM)
VMEM = pl.BlockSpec(memory_space=pltpu.VMEM)
HBM = pl.BlockSpec(memory_space=pltpu.HBM)
SWAP = [(0, 1), (1, 0)]
LAYERS = ("zh", "c", "zl")


def call(kernel, flops, out_shape, scalars, arrays, halves=(), scratch=(), mib=16):
    if halves:
        held = pltpu.VMEM((len(halves), *halves[0].shape), BF16)
        scratch = (held, pltpu.SemaphoreType.DMA((len(halves),)), *scratch)
    return pl.pallas_call(
        kernel,
        out_shape=out_shape,
        in_specs=[SMEM] * len(scalars) + [VMEM] * len(arrays) + [HBM] * len(halves),
        out_specs=(VMEM,) * len(out_shape),
        scratch_shapes=list(scratch),
        compiler_params=pltpu.CompilerParams(vmem_limit_bytes=mib << 20),
        cost_estimate=pl.CostEstimate(flops=flops, bytes_accessed=6 << 20, transcendentals=0),
        name=kernel.__name__,
    )(*scalars, *arrays, *halves)


def per_device(
    tokens, grad_out, gate_tiles, up_tiles, down_tiles, gate_index, up_index, down_index
):
    here, width = tokens.shape
    line = lax.axis_size("x")
    rows, slots = here * line, gate_tiles.shape[1]
    blocks, hidden = width // TILE, 8
    pairs = lax.axis_size(DP) // 2
    gw, uw, dw = gate_tiles[0], up_tiles[0], down_tiles[0]
    at_core = lax.axis_index("c").astype(jnp.int32)
    core = at_core.reshape(1)
    with jax.named_scope("gather"):
        both = jnp.concatenate([tokens, grad_out], axis=1)
        send = jnp.broadcast_to(both[None], (line, here, 2 * width))
        xa = lax.all_to_all(send, "x", 0, 0, tiled=True).reshape(rows, 2 * width)
    with jax.named_scope("weights"):
        part_of = lambda w: lax.dynamic_slice_in_dim(w, at_core * (slots // 2), slots // 2)
        stack = jnp.stack([part_of(w) for w in (gw, uw, dw)])
        index = jnp.concatenate([gate_index, up_index, down_index], axis=1)
        stack, index = lax.optimization_barrier((stack, index))
        far = lax.ppermute(index, "zl", SWAP)
        ra = lax.ppermute(stack, LAYERS, beside())
        ra, far = lax.optimization_barrier((ra, far))
        rb = lax.ppermute(ra, "c", SWAP)
    own = (gate_index, up_index, down_index)
    work = 2 * rows * TILE * TILE * 2 * slots
    shape = lambda *dims: jax.ShapeDtypeStruct(dims, BF16)
    dgate, dup, hid = call(
        forward,
        3 * work,
        (shape(hidden, rows, TILE),) * 3,
        (*own, far, core),
        (xa, gw, uw, dw),
        (ra, rb),
        [pltpu.VMEM((hidden, rows, TILE), F32)] * 3,
    )
    (part,) = call(
        back,
        2 * work,
        (jax.ShapeDtypeStruct((rows, width), F32),),
        (*own[:2], far, core),
        (dgate, dup, gw, uw),
        (ra, rb),
        [pltpu.VMEM((blocks, rows, TILE), F32)],
    )
    own_mine, own_theirs, far_mine, far_theirs = call(
        tile_terms,
        3 * work,
        (shape(pairs, 32, 3 * TILE),) * 4,
        (*own, far, core),
        (xa, dgate, dup, hid),
    )
    own_mine, _ = lax.optimization_barrier((own_mine, part))
    with jax.named_scope("partials"):
        input_sum = lax.psum_scatter(part, "x", scatter_dimension=0, tiled=True).astype(BF16)
    add = lambda *terms: sum(t.astype(F32) for t in terms).astype(BF16)
    with jax.named_scope("cores"):
        far_got = lax.ppermute(far_theirs, "c", SWAP)
        own_got = lax.ppermute(own_theirs, "c", SWAP)
    with jax.named_scope("layers"):
        near = lax.ppermute(add(far_mine, far_got), LAYERS, beside())
    with jax.named_scope("tile_sums"):
        grads = lax.all_to_all(add(own_mine, own_got, near), ("zh", "y"), 0, 0, tiled=True)
        sums = jnp.sum(grads.astype(F32), axis=0)
    return (input_sum, sums[None])


def solution(mesh):
    fine = Mesh(mesh.devices.reshape(4, 8, 2, 2, 8), DP + TEN)
    both = P(DP + TEN, None)
    return jax.shard_map(
        per_device,
        mesh=fine,
        in_specs=(both, both)
        + (P(TEN, None, None, None),) * 3
        + (P(TEN, None),) * 3,
        out_specs=(both, P(TEN, DP, None)),
        check_vma=False,
    )
```

```python
import jax
import jax.numpy as jnp
from jax import lax
from jax.experimental import pallas as pl
from jax.experimental.pallas import tpu as pltpu
from jax.sharding import Mesh, PartitionSpec as P

TILE = 128
DP = ("zh", "y", "c")
TEN = ("zl", "x")
F32 = jnp.float32
BF16 = jnp.bfloat16


def lanes(ref, tile_at):
    return ref[:, pl.ds(pl.multiple_of(tile_at * TILE, TILE), TILE)]


def dot(left, right, on):
    return lax.dot_general(left, right, ((on[:1], on[1:]), ((), ())), preferred_element_type=F32)


def fetch(halves, held, sems):
    copies = [pltpu.make_async_copy(r, held.at[h], sems.at[h]) for h, r in enumerate(halves)]
    for copy in copies:
        copy.start()
    return copies


def slot_list(core, own, far, own_w, held, copies):
    slots = own_w[0].shape[0]
    half = slots // 2
    for s in range(slots):
        yield 0, [i[0, s] for i in own], [w.at[s] for w in own_w]
    for j in range(slots):
        h, k = divmod(j, half)
        if k == 0:
            copies[h].wait()
        at = (core if h == 0 else 1 - core) * half + k
        yield 1, [far[0, n * slots + at] for n in range(3)], [held.at[h, n, k] for n in range(3)]


def forward(
    g_idx, u_idx, d_idx, far, core, xa, gw, uw, dw, ra, rb, dgate, dup, hid, held, sems, gate, up, dhid
):
    copies = fetch((ra, rb), held, sems)
    blocks = xa.shape[1] // TILE // 2
    hidden = gate.shape[0] // 2
    for acc in (gate, up, dhid):
        acc[...] = jnp.zeros_like(acc)
    slots = slot_list(core[0], (g_idx, u_idx, d_idx), far, (gw, uw, dw), held, copies)
    for side, (gv, uv, dv), (g_t, u_t, d_t) in slots:
        for v, w, acc in ((gv, g_t, gate), (uv, u_t, up)):
            safe = jnp.maximum(v, 0)
            val = dot(lanes(xa, safe >> 2), w[...], (1, 0))
            acc[side * hidden + (safe & 3)] += jnp.where(v >= 0, val, 0.0)
        safe = jnp.maximum(dv, 0)
        val = dot(lanes(xa, blocks + (safe & 31)), d_t[...], (1, 1))
        dhid[side * hidden + (safe >> 5)] += jnp.where(dv >= 0, val, 0.0)
    for b in range(gate.shape[0]):
        g, u, dh = gate[b], up[b], dhid[b]
        sig = jax.nn.sigmoid(g)
        act = g * sig
        hid[b] = (act * u).astype(BF16)
        dgate[b] = (dh * u * sig * (1.0 + g * (1.0 - sig))).astype(BF16)
        dup[b] = (dh * act).astype(BF16)


def back(g_idx, u_idx, far, core, place, dgate, dup, gw, uw, ra, rb, *rest):
    parts, (held, sems, acc) = rest[:-3], rest[-3:]
    copies = fetch((ra, rb), held, sems)
    hidden = dgate.shape[0] // 2
    acc[...] = jnp.zeros_like(acc)
    slots = slot_list(core[0], (g_idx, u_idx, u_idx), far, (gw, uw, uw), held, copies)
    for side, vs, ws in slots:
        for v, w, grad in zip(vs[:2], ws[:2], (dgate, dup)):
            safe = jnp.maximum(v, 0)
            val = dot(grad[side * hidden + (safe & 3)], w[...], (1, 1))
            acc[safe >> 2] += jnp.where(v >= 0, val, 0.0)
    here = parts[0].shape[0]
    for d, part in enumerate(parts):
        at = pl.multiple_of(((place[0] + d) & (len(parts) - 1)) * here, here)
        for b in range(acc.shape[0]):
            part[:, b * TILE : (b + 1) * TILE] = acc[b, pl.ds(at, here), :].astype(BF16)


def tile_terms(
    g_idx, u_idx, d_idx, far, core, xa, dgate, dup, hid, own_mine, own_theirs, far_mine, far_theirs
):
    blocks = xa.shape[1] // TILE // 2
    hidden = dgate.shape[0] // 2
    first = core[0] == 0
    sets = (
        (1, lambda n, s: far[0, n * CAP + s], far_mine, far_theirs),
        (0, lambda n, s: (g_idx, u_idx, d_idx)[n][0, s], own_mine, own_theirs),
    )
    for side, index, mine, theirs in sets:
        for slot in range(CAP):
            outs = []
            for n, grad in ((0, dgate), (1, dup)):
                v = index(n, slot)
                safe = jnp.maximum(v, 0)
                val = dot(lanes(xa, safe >> 2), grad[side * hidden + (safe & 3)], (0, 0))
                outs.append(jnp.where(v >= 0, val, 0.0))
            v = index(2, slot)
            safe = jnp.maximum(v, 0)
            val = dot(hid[side * hidden + (safe >> 5)], lanes(xa, blocks + (safe & 31)), (0, 0))
            outs.append(jnp.where(v >= 0, val, 0.0))
            for k, val in enumerate(outs):
                for half in range(2):
                    even = val[64 * half : 64 * half + 32]
                    odd = val[64 * half + 32 : 64 * half + 64]
                    at = (2 * slot + half, slice(None), slice(k * TILE, (k + 1) * TILE))
                    mine[at] = jnp.where(first, even, odd).astype(BF16)
                    theirs[at] = jnp.where(first, odd, even).astype(BF16)


def beside():
    pairs = []
    for zh in range(4):
        for c in range(2):
            for zl in range(2):
                to = (zh if c == 0 else (zh + (1 if zl else -1)) % 4, c, 1 - zl)
                pairs.append(((zh * 2 + c) * 2 + zl, (to[0] * 2 + to[1]) * 2 + to[2]))
    return pairs


CAP = 16

SMEM = pl.BlockSpec(memory_space=pltpu.SMEM)
VMEM = pl.BlockSpec(memory_space=pltpu.VMEM)
HBM = pl.BlockSpec(memory_space=pltpu.HBM)
SWAP = [(0, 1), (1, 0)]
LAYERS = ("zh", "c", "zl")


def call(kernel, flops, out_shape, scalars, arrays, halves=(), scratch=(), mib=16):
    if halves:
        held = pltpu.VMEM((len(halves), *halves[0].shape), BF16)
        scratch = (held, pltpu.SemaphoreType.DMA((len(halves),)), *scratch)
    return pl.pallas_call(
        kernel,
        out_shape=out_shape,
        in_specs=[SMEM] * len(scalars) + [VMEM] * len(arrays) + [HBM] * len(halves),
        out_specs=(VMEM,) * len(out_shape),
        scratch_shapes=list(scratch),
        compiler_params=pltpu.CompilerParams(vmem_limit_bytes=mib << 20),
        cost_estimate=pl.CostEstimate(flops=flops, bytes_accessed=6 << 20, transcendentals=0),
        name=kernel.__name__,
    )(*scalars, *arrays, *halves)


def per_device(
    tokens, grad_out, gate_tiles, up_tiles, down_tiles, gate_index, up_index, down_index
):
    here, width = tokens.shape
    line = lax.axis_size("x")
    rows, slots = here * line, gate_tiles.shape[1]
    blocks, hidden = width // TILE, 8
    pairs = lax.axis_size(DP) // 2
    gw, uw, dw = gate_tiles[0], up_tiles[0], down_tiles[0]
    at_core = lax.axis_index("c").astype(jnp.int32)
    core = at_core.reshape(1)
    with jax.named_scope("gather"):
        both = jnp.concatenate([tokens, grad_out], axis=1)
        send = jnp.broadcast_to(both[None], (line, here, 2 * width))
        xa = lax.all_to_all(send, "x", 0, 0, tiled=True).reshape(rows, 2 * width)
    with jax.named_scope("weights"):
        part_of = lambda w: lax.dynamic_slice_in_dim(w, at_core * (slots // 2), slots // 2)
        stack = jnp.stack([part_of(w) for w in (gw, uw, dw)])
        index = jnp.concatenate([gate_index, up_index, down_index], axis=1)
        stack, index = lax.optimization_barrier((stack, index))
        far = lax.ppermute(index, "zl", SWAP)
        ra = lax.ppermute(stack, LAYERS, beside())
        ra, far = lax.optimization_barrier((ra, far))
        rb = lax.ppermute(ra, "c", SWAP)
    own = (gate_index, up_index, down_index)
    work = 2 * rows * TILE * TILE * 2 * slots
    shape = lambda *dims: jax.ShapeDtypeStruct(dims, BF16)
    dgate, dup, hid = call(
        forward,
        3 * work,
        (shape(hidden, rows, TILE),) * 3,
        (*own, far, core),
        (xa, gw, uw, dw),
        (ra, rb),
        [pltpu.VMEM((hidden, rows, TILE), F32)] * 3,
    )
    parts = call(
        back,
        2 * work,
        (shape(here, width),) * line,
        (*own[:2], far, core, lax.axis_index("x").astype(jnp.int32).reshape(1)),
        (dgate, dup, gw, uw),
        (ra, rb),
        [pltpu.VMEM((blocks, rows, TILE), F32)],
    )
    own_mine, own_theirs, far_mine, far_theirs = call(
        tile_terms,
        3 * work,
        (shape(pairs, 32, 3 * TILE),) * 4,
        (*own, far, core),
        (xa, dgate, dup, hid),
    )
    own_mine, _ = lax.optimization_barrier((own_mine, parts[0]))
    add = lambda *terms: sum(t.astype(F32) for t in terms).astype(BF16)
    with jax.named_scope("partials"):
        ring = lambda d: [(i, (i + d) % line) for i in range(line)]
        came = [lax.ppermute(parts[d], "x", ring(d)) for d in range(1, line)]
        input_sum = add(parts[0], *came)
    with jax.named_scope("cores"):
        far_got = lax.ppermute(far_theirs, "c", SWAP)
        own_got = lax.ppermute(own_theirs, "c", SWAP)
    with jax.named_scope("layers"):
        near = lax.ppermute(add(far_mine, far_got), LAYERS, beside())
    with jax.named_scope("tile_sums"):
        grads = lax.all_to_all(add(own_mine, own_got, near), ("zh", "y"), 0, 0, tiled=True)
        sums = jnp.sum(grads.astype(F32), axis=0)
    return (input_sum, sums[None])


def solution(mesh):
    fine = Mesh(mesh.devices.reshape(4, 8, 2, 2, 8), DP + TEN)
    both = P(DP + TEN, None)
    return jax.shard_map(
        per_device,
        mesh=fine,
        in_specs=(both, both)
        + (P(TEN, None, None, None),) * 3
        + (P(TEN, None),) * 3,
        out_specs=(both, P(TEN, DP, None)),
        check_vma=False,
    )
```

```python
import jax
import jax.numpy as jnp
from jax import lax
from jax.experimental import pallas as pl
from jax.experimental.pallas import tpu as pltpu
from jax.sharding import Mesh, PartitionSpec as P

TILE = 128
DP = ("zh", "y", "c")
TEN = ("zl", "x")
F32 = jnp.float32
BF16 = jnp.bfloat16


def lanes(ref, tile_at):
    return ref[:, pl.ds(pl.multiple_of(tile_at * TILE, TILE), TILE)]


def dot(left, right, on):
    return lax.dot_general(left, right, ((on[:1], on[1:]), ((), ())), preferred_element_type=F32)


def fetch(halves, held, sems):
    copies = [pltpu.make_async_copy(r, held.at[h], sems.at[h]) for h, r in enumerate(halves)]
    for copy in copies:
        copy.start()
    return copies


def slot_list(core, own, far, own_w, held, copies):
    slots = own_w[0].shape[0]
    half = slots // 2
    for s in range(slots):
        yield 0, [i[0, s] for i in own], [w.at[s] for w in own_w]
    for j in range(slots):
        h, k = divmod(j, half)
        if k == 0:
            copies[h].wait()
        at = (core if h == 0 else 1 - core) * half + k
        yield 1, [far[0, n * slots + at] for n in range(3)], [held.at[h, n, k] for n in range(3)]


def forward(
    g_idx, u_idx, d_idx, far, core, xa, gw, uw, dw, ra, rb, dgate, dup, hid, held, sems, gate, up, dhid
):
    copies = fetch((ra, rb), held, sems)
    blocks = xa.shape[1] // TILE // 2
    hidden = gate.shape[0] // 2
    for acc in (gate, up, dhid):
        acc[...] = jnp.zeros_like(acc)
    slots = slot_list(core[0], (g_idx, u_idx, d_idx), far, (gw, uw, dw), held, copies)
    for side, (gv, uv, dv), (g_t, u_t, d_t) in slots:
        for v, w, acc in ((gv, g_t, gate), (uv, u_t, up)):
            safe = jnp.maximum(v, 0)
            val = dot(lanes(xa, safe >> 2), w[...], (1, 0))
            acc[side * hidden + (safe & 3)] += jnp.where(v >= 0, val, 0.0)
        safe = jnp.maximum(dv, 0)
        val = dot(lanes(xa, blocks + (safe & 31)), d_t[...], (1, 1))
        dhid[side * hidden + (safe >> 5)] += jnp.where(dv >= 0, val, 0.0)
    for b in range(gate.shape[0]):
        g, u, dh = gate[b], up[b], dhid[b]
        sig = jax.nn.sigmoid(g)
        act = g * sig
        hid[b] = (act * u).astype(BF16)
        dgate[b] = (dh * u * sig * (1.0 + g * (1.0 - sig))).astype(BF16)
        dup[b] = (dh * act).astype(BF16)


def back(g_idx, u_idx, far, core, place, dgate, dup, gw, uw, ra, rb, give, *rest):
    keep, (held, sems, acc) = rest[:-3], rest[-3:]
    copies = fetch((ra, rb), held, sems)
    hidden = dgate.shape[0] // 2
    acc[...] = jnp.zeros_like(acc)
    slots = slot_list(core[0], (g_idx, u_idx, u_idx), far, (gw, uw, uw), held, copies)
    for side, vs, ws in slots:
        for v, w, grad in zip(vs[:2], ws[:2], (dgate, dup)):
            safe = jnp.maximum(v, 0)
            val = dot(grad[side * hidden + (safe & 3)], w[...], (1, 1))
            acc[safe >> 2] += jnp.where(v >= 0, val, 0.0)
    here = keep[0].shape[0]
    me = place[0]
    near = me + 1 - 2 * (me & 1)
    for k in range(len(keep)):
        row = lambda x: pl.ds(pl.multiple_of(((x + 2 * k) & (2 * len(keep) - 1)) * here, here), here)
        for b in range(acc.shape[0]):
            at = slice(b * TILE, (b + 1) * TILE)
            give[k, :, at] = acc[b, row(near), :].astype(BF16)
            keep[k][:, at] = acc[b, row(me), :].astype(BF16)


def tile_terms(
    g_idx, u_idx, d_idx, far, core, xa, dgate, dup, hid, own_mine, own_theirs, far_mine, far_theirs
):
    blocks = xa.shape[1] // TILE // 2
    hidden = dgate.shape[0] // 2
    first = core[0] == 0
    sets = (
        (1, lambda n, s: far[0, n * CAP + s], far_mine, far_theirs),
        (0, lambda n, s: (g_idx, u_idx, d_idx)[n][0, s], own_mine, own_theirs),
    )
    for side, index, mine, theirs in sets:
        for slot in range(CAP):
            outs = []
            for n, grad in ((0, dgate), (1, dup)):
                v = index(n, slot)
                safe = jnp.maximum(v, 0)
                val = dot(lanes(xa, safe >> 2), grad[side * hidden + (safe & 3)], (0, 0))
                outs.append(jnp.where(v >= 0, val, 0.0))
            v = index(2, slot)
            safe = jnp.maximum(v, 0)
            val = dot(hid[side * hidden + (safe >> 5)], lanes(xa, blocks + (safe & 31)), (0, 0))
            outs.append(jnp.where(v >= 0, val, 0.0))
            for k, val in enumerate(outs):
                for half in range(2):
                    even = val[64 * half : 64 * half + 32]
                    odd = val[64 * half + 32 : 64 * half + 64]
                    at = (2 * slot + half, slice(None), slice(k * TILE, (k + 1) * TILE))
                    mine[at] = jnp.where(first, even, odd).astype(BF16)
                    theirs[at] = jnp.where(first, odd, even).astype(BF16)


def beside():
    pairs = []
    for zh in range(4):
        for c in range(2):
            for zl in range(2):
                to = (zh if c == 0 else (zh + (1 if zl else -1)) % 4, c, 1 - zl)
                pairs.append(((zh * 2 + c) * 2 + zl, (to[0] * 2 + to[1]) * 2 + to[2]))
    return pairs


CAP = 16

SMEM = pl.BlockSpec(memory_space=pltpu.SMEM)
VMEM = pl.BlockSpec(memory_space=pltpu.VMEM)
HBM = pl.BlockSpec(memory_space=pltpu.HBM)
SWAP = [(0, 1), (1, 0)]
LAYERS = ("zh", "c", "zl")


def call(kernel, flops, out_shape, scalars, arrays, halves=(), scratch=(), mib=16):
    if halves:
        held = pltpu.VMEM((len(halves), *halves[0].shape), BF16)
        scratch = (held, pltpu.SemaphoreType.DMA((len(halves),)), *scratch)
    return pl.pallas_call(
        kernel,
        out_shape=out_shape,
        in_specs=[SMEM] * len(scalars) + [VMEM] * len(arrays) + [HBM] * len(halves),
        out_specs=(VMEM,) * len(out_shape),
        scratch_shapes=list(scratch),
        compiler_params=pltpu.CompilerParams(vmem_limit_bytes=mib << 20),
        cost_estimate=pl.CostEstimate(flops=flops, bytes_accessed=6 << 20, transcendentals=0),
        name=kernel.__name__,
    )(*scalars, *arrays, *halves)


def per_device(
    tokens, grad_out, gate_tiles, up_tiles, down_tiles, gate_index, up_index, down_index
):
    here, width = tokens.shape
    line = lax.axis_size("x")
    rows, slots = here * line, gate_tiles.shape[1]
    blocks, hidden = width // TILE, 8
    pairs = lax.axis_size(DP) // 2
    gw, uw, dw = gate_tiles[0], up_tiles[0], down_tiles[0]
    at_core = lax.axis_index("c").astype(jnp.int32)
    core = at_core.reshape(1)
    with jax.named_scope("gather"):
        both = jnp.concatenate([tokens, grad_out], axis=1)
        send = jnp.broadcast_to(both[None], (line, here, 2 * width))
        xa = lax.all_to_all(send, "x", 0, 0, tiled=True).reshape(rows, 2 * width)
    with jax.named_scope("weights"):
        part_of = lambda w: lax.dynamic_slice_in_dim(w, at_core * (slots // 2), slots // 2)
        stack = jnp.stack([part_of(w) for w in (gw, uw, dw)])
        index = jnp.concatenate([gate_index, up_index, down_index], axis=1)
        stack, index = lax.optimization_barrier((stack, index))
        far = lax.ppermute(index, "zl", SWAP)
        ra = lax.ppermute(stack, LAYERS, beside())
        ra, far = lax.optimization_barrier((ra, far))
        rb = lax.ppermute(ra, "c", SWAP)
    own = (gate_index, up_index, down_index)
    work = 2 * rows * TILE * TILE * 2 * slots
    shape = lambda *dims: jax.ShapeDtypeStruct(dims, BF16)
    dgate, dup, hid = call(
        forward,
        3 * work,
        (shape(hidden, rows, TILE),) * 3,
        (*own, far, core),
        (xa, gw, uw, dw),
        (ra, rb),
        [pltpu.VMEM((hidden, rows, TILE), F32)] * 3,
    )
    give, *keep = call(
        back,
        2 * work,
        (shape(line // 2, here, width),) + (shape(here, width),) * (line // 2),
        (*own[:2], far, core, lax.axis_index("x").astype(jnp.int32).reshape(1)),
        (dgate, dup, gw, uw),
        (ra, rb),
        [pltpu.VMEM((blocks, rows, TILE), F32)],
    )
    own_mine, own_theirs, far_mine, far_theirs = call(
        tile_terms,
        3 * work,
        (shape(pairs, 32, 3 * TILE),) * 4,
        (*own, far, core),
        (xa, dgate, dup, hid),
    )
    add = lambda *terms: sum(t.astype(F32) for t in terms).astype(BF16)
    with jax.named_scope("partials"):
        got = lax.ppermute(give, "x", [(i, i ^ 1) for i in range(line)])
        pair = [add(keep[k], got[k]) for k in range(line // 2)]
        ring = lambda d: [(i, (i + d) % line) for i in range(line)]
        came = [lax.ppermute(pair[k], "x", ring(2 * k)) for k in (1, 3, 2)]
        input_sum = add(*[t.astype(F32) for t in (keep[0], got[0])], *came)
    own_mine, got = lax.optimization_barrier((own_mine, got))
    with jax.named_scope("cores"):
        far_got = lax.ppermute(far_theirs, "c", SWAP)
        own_got = lax.ppermute(own_theirs, "c", SWAP)
    with jax.named_scope("layers"):
        near = lax.ppermute(add(far_mine, far_got), LAYERS, beside())
    with jax.named_scope("tile_sums"):
        grads = lax.all_to_all(add(own_mine, own_got, near), ("zh", "y"), 0, 0, tiled=True)
        sums = jnp.sum(grads.astype(F32), axis=0)
    return (input_sum, sums[None])


def solution(mesh):
    fine = Mesh(mesh.devices.reshape(4, 8, 2, 2, 8), DP + TEN)
    both = P(DP + TEN, None)
    return jax.shard_map(
        per_device,
        mesh=fine,
        in_specs=(both, both)
        + (P(TEN, None, None, None),) * 3
        + (P(TEN, None),) * 3,
        out_specs=(both, P(TEN, DP, None)),
        check_vma=False,
    )
```

```python
import jax
import jax.numpy as jnp
from jax import lax
from jax.experimental import pallas as pl
from jax.experimental.pallas import tpu as pltpu
from jax.sharding import Mesh, PartitionSpec as P

TILE = 128
DP = ("zh", "y", "c")
TEN = ("zl", "x")
F32 = jnp.float32
BF16 = jnp.bfloat16


def lanes(ref, tile_at):
    return ref[:, pl.ds(pl.multiple_of(tile_at * TILE, TILE), TILE)]


def dot(left, right, on):
    return lax.dot_general(left, right, ((on[:1], on[1:]), ((), ())), preferred_element_type=F32)


def fetch(halves, held, sems):
    copies = [pltpu.make_async_copy(r, held.at[h], sems.at[h]) for h, r in enumerate(halves)]
    for copy in copies:
        copy.start()
    return copies


def slot_list(core, own, far, own_w, held, copies):
    slots = own_w[0].shape[0]
    half = slots // 2
    for s in range(slots):
        yield 0, [i[0, s] for i in own], [w.at[s] for w in own_w]
    for j in range(slots):
        h, k = divmod(j, half)
        if k == 0:
            copies[h].wait()
        at = (core if h == 0 else 1 - core) * half + k
        yield 1, [far[0, n * slots + at] for n in range(3)], [held.at[h, n, k] for n in range(3)]


def forward(
    g_idx, u_idx, d_idx, far, core, xa, gw, uw, dw, ra, rb, dgate, dup, hid, held, sems, gate, up, dhid
):
    copies = fetch((ra, rb), held, sems)
    blocks = xa.shape[1] // TILE // 2
    hidden = gate.shape[0] // 2
    for acc in (gate, up, dhid):
        acc[...] = jnp.zeros_like(acc)
    slots = slot_list(core[0], (g_idx, u_idx, d_idx), far, (gw, uw, dw), held, copies)
    for side, (gv, uv, dv), (g_t, u_t, d_t) in slots:
        for v, w, acc in ((gv, g_t, gate), (uv, u_t, up)):
            safe = jnp.maximum(v, 0)
            val = dot(lanes(xa, safe >> 2), w[...], (1, 0))
            acc[side * hidden + (safe & 3)] += jnp.where(v >= 0, val, 0.0)
        safe = jnp.maximum(dv, 0)
        val = dot(lanes(xa, blocks + (safe & 31)), d_t[...], (1, 1))
        dhid[side * hidden + (safe >> 5)] += jnp.where(dv >= 0, val, 0.0)
    for b in range(gate.shape[0]):
        g, u, dh = gate[b], up[b], dhid[b]
        sig = jax.nn.sigmoid(g)
        act = g * sig
        hid[b] = (act * u).astype(BF16)
        dgate[b] = (dh * u * sig * (1.0 + g * (1.0 - sig))).astype(BF16)
        dup[b] = (dh * act).astype(BF16)


def back(g_idx, u_idx, far, core, place, dgate, dup, gw, uw, ra, rb, give, *rest):
    keep, (held, sems, acc) = rest[:-3], rest[-3:]
    copies = fetch((ra, rb), held, sems)
    hidden = dgate.shape[0] // 2
    acc[...] = jnp.zeros_like(acc)
    slots = slot_list(core[0], (g_idx, u_idx, u_idx), far, (gw, uw, uw), held, copies)
    for side, vs, ws in slots:
        for v, w, grad in zip(vs[:2], ws[:2], (dgate, dup)):
            safe = jnp.maximum(v, 0)
            val = dot(grad[side * hidden + (safe & 3)], w[...], (1, 1))
            acc[safe >> 2] += jnp.where(v >= 0, val, 0.0)
    here = keep[0].shape[0]
    me = place[0]
    near = me + 1 - 2 * (me & 1)
    for k in range(len(keep)):
        row = lambda x: pl.ds(pl.multiple_of(((x + 2 * k) & (2 * len(keep) - 1)) * here, here), here)
        for b in range(acc.shape[0]):
            at = slice(b * TILE, (b + 1) * TILE)
            give[k, :, at] = acc[b, row(near), :].astype(BF16)
            keep[k][:, at] = acc[b, row(me), :].astype(BF16)


def terms(side, index, core, xa, dgate, dup, hid, mine, theirs):
    blocks = xa.shape[1] // TILE // 2
    hidden = dgate.shape[0] // 2
    first = core[0] == 0
    for slot in range(CAP):
        outs = []
        for n, grad in ((0, dgate), (1, dup)):
            v = index(n, slot)
            safe = jnp.maximum(v, 0)
            val = dot(lanes(xa, safe >> 2), grad[side * hidden + (safe & 3)], (0, 0))
            outs.append(jnp.where(v >= 0, val, 0.0))
        v = index(2, slot)
        safe = jnp.maximum(v, 0)
        val = dot(hid[side * hidden + (safe >> 5)], lanes(xa, blocks + (safe & 31)), (0, 0))
        outs.append(jnp.where(v >= 0, val, 0.0))
        for k, val in enumerate(outs):
            for half in range(2):
                even = val[64 * half : 64 * half + 32]
                odd = val[64 * half + 32 : 64 * half + 64]
                at = (2 * slot + half, slice(None), slice(k * TILE, (k + 1) * TILE))
                mine[at] = jnp.where(first, even, odd).astype(BF16)
                theirs[at] = jnp.where(first, odd, even).astype(BF16)


def far_terms(far, core, *refs):
    terms(1, lambda n, s: far[0, n * CAP + s], core, *refs)


def own_terms(g_idx, u_idx, d_idx, core, *refs):
    terms(0, lambda n, s: (g_idx, u_idx, d_idx)[n][0, s], core, *refs)


def total(*refs):
    *parts, out = refs
    for k in range(out.shape[0]):
        val = parts[0][k].astype(F32)
        for t in parts[1:]:
            val += t[k].astype(F32)
        out[k] = val.astype(BF16)


def beside():
    pairs = []
    for zh in range(4):
        for c in range(2):
            for zl in range(2):
                to = (zh if c == 0 else (zh + (1 if zl else -1)) % 4, c, 1 - zl)
                pairs.append(((zh * 2 + c) * 2 + zl, (to[0] * 2 + to[1]) * 2 + to[2]))
    return pairs


CAP = 16

SMEM = pl.BlockSpec(memory_space=pltpu.SMEM)
VMEM = pl.BlockSpec(memory_space=pltpu.VMEM)
HBM = pl.BlockSpec(memory_space=pltpu.HBM)
SWAP = [(0, 1), (1, 0)]
LAYERS = ("zh", "c", "zl")


def call(kernel, flops, out_shape, scalars, arrays, halves=(), scratch=(), mib=16):
    if halves:
        held = pltpu.VMEM((len(halves), *halves[0].shape), BF16)
        scratch = (held, pltpu.SemaphoreType.DMA((len(halves),)), *scratch)
    return pl.pallas_call(
        kernel,
        out_shape=out_shape,
        in_specs=[SMEM] * len(scalars) + [VMEM] * len(arrays) + [HBM] * len(halves),
        out_specs=(VMEM,) * len(out_shape),
        scratch_shapes=list(scratch),
        compiler_params=pltpu.CompilerParams(vmem_limit_bytes=mib << 20),
        cost_estimate=pl.CostEstimate(flops=flops, bytes_accessed=6 << 20, transcendentals=0),
        name=kernel.__name__,
    )(*scalars, *arrays, *halves)


def per_device(
    tokens, grad_out, gate_tiles, up_tiles, down_tiles, gate_index, up_index, down_index
):
    here, width = tokens.shape
    line = lax.axis_size("x")
    rows, slots = here * line, gate_tiles.shape[1]
    blocks, hidden = width // TILE, 8
    pairs = lax.axis_size(DP) // 2
    gw, uw, dw = gate_tiles[0], up_tiles[0], down_tiles[0]
    at_core = lax.axis_index("c").astype(jnp.int32)
    core = at_core.reshape(1)
    with jax.named_scope("gather"):
        both = jnp.concatenate([tokens, grad_out], axis=1)
        send = jnp.broadcast_to(both[None], (line, here, 2 * width))
        xa = lax.all_to_all(send, "x", 0, 0, tiled=True).reshape(rows, 2 * width)
    with jax.named_scope("weights"):
        part_of = lambda w: lax.dynamic_slice_in_dim(w, at_core * (slots // 2), slots // 2)
        stack = jnp.stack([part_of(w) for w in (gw, uw, dw)])
        index = jnp.concatenate([gate_index, up_index, down_index], axis=1)
        stack, index = lax.optimization_barrier((stack, index))
        far = lax.ppermute(index, "zl", SWAP)
        ra = lax.ppermute(stack, LAYERS, beside())
        ra, far = lax.optimization_barrier((ra, far))
        rb = lax.ppermute(ra, "c", SWAP)
    own = (gate_index, up_index, down_index)
    work = 2 * rows * TILE * TILE * 2 * slots
    shape = lambda *dims: jax.ShapeDtypeStruct(dims, BF16)
    dgate, dup, hid = call(
        forward,
        3 * work,
        (shape(hidden, rows, TILE),) * 3,
        (*own, far, core),
        (xa, gw, uw, dw),
        (ra, rb),
        [pltpu.VMEM((hidden, rows, TILE), F32)] * 3,
    )
    half_terms = (shape(pairs, 32, 3 * TILE),) * 2
    far_mine, far_theirs = call(
        far_terms, 3 * work // 2, half_terms, (far, core), (xa, dgate, dup, hid)
    )
    with jax.named_scope("cores"):
        far_got = lax.ppermute(far_theirs, "c", SWAP)
    own_mine, own_theirs = call(
        own_terms, 3 * work // 2, half_terms, (*own, core), (xa, dgate, dup, hid)
    )
    own_mine, far_got = lax.optimization_barrier((own_mine, far_got))
    with jax.named_scope("layers"):
        (far_sum,) = call(total, 0, half_terms[:1], (), (far_mine, far_got))
        near = lax.ppermute(far_sum, LAYERS, beside())
    give, *keep = call(
        back,
        2 * work,
        (shape(line // 2, here, width),) + (shape(here, width),) * (line // 2),
        (*own[:2], far, core, lax.axis_index("x").astype(jnp.int32).reshape(1)),
        (dgate, dup, gw, uw),
        (ra, rb),
        [pltpu.VMEM((blocks, rows, TILE), F32)],
    )
    add = lambda *addends: sum(t.astype(F32) for t in addends).astype(BF16)
    with jax.named_scope("partials"):
        got = lax.ppermute(give, "x", [(i, i ^ 1) for i in range(line)])
        pair = [add(keep[k], got[k]) for k in range(line // 2)]
        ring = lambda d: [(i, (i + d) % line) for i in range(line)]
        came = [lax.ppermute(pair[k], "x", ring(2 * k)) for k in (1, 3, 2)]
        input_sum = add(keep[0], got[0], *came)
    with jax.named_scope("tile_sums"):
        own_got = lax.ppermute(own_theirs, "c", SWAP)
        own_mine, got = lax.optimization_barrier((own_mine, got))
        (all_sum,) = call(total, 0, half_terms[:1], (), (own_mine, own_got, near))
        grads = lax.all_to_all(all_sum, ("zh", "y"), 0, 0, tiled=True)
        sums = jnp.sum(grads.astype(F32), axis=0)
    return (input_sum, sums[None])


def solution(mesh):
    fine = Mesh(mesh.devices.reshape(4, 8, 2, 2, 8), DP + TEN)
    both = P(DP + TEN, None)
    return jax.shard_map(
        per_device,
        mesh=fine,
        in_specs=(both, both)
        + (P(TEN, None, None, None),) * 3
        + (P(TEN, None),) * 3,
        out_specs=(both, P(TEN, DP, None)),
        check_vma=False,
    )
```

```python
import jax
import jax.numpy as jnp
from jax import lax
from jax.experimental import pallas as pl
from jax.experimental.pallas import tpu as pltpu
from jax.sharding import Mesh, PartitionSpec as P

TILE = 128
DP = ("zh", "y", "c")
TEN = ("zl", "x")
F32 = jnp.float32
BF16 = jnp.bfloat16


def lanes(ref, tile_at):
    return ref[:, pl.ds(pl.multiple_of(tile_at * TILE, TILE), TILE)]


def dot(left, right, on):
    return lax.dot_general(left, right, ((on[:1], on[1:]), ((), ())), preferred_element_type=F32)


def spread(tokens, grad_out, out, sems):
    width = tokens.shape[1]
    copies = [
        pltpu.make_async_copy(t, out.at[n, :, pl.ds(k * width, width)], sems.at[n, k])
        for n in range(out.shape[0])
        for k, t in enumerate((tokens, grad_out))
    ]
    for copy in copies:
        copy.start()
    for copy in copies:
        copy.wait()


def fetch(halves, held, sems):
    copies = [pltpu.make_async_copy(r, held.at[h], sems.at[h]) for h, r in enumerate(halves)]
    for copy in copies:
        copy.start()
    return copies


def slot_list(core, own, far, own_w, held, copies):
    slots = own_w[0].shape[0]
    half = slots // 2
    for s in range(slots):
        yield 0, [i[0, s] for i in own], [w.at[s] for w in own_w]
    for j in range(slots):
        h, k = divmod(j, half)
        if k == 0:
            copies[h].wait()
        at = (core if h == 0 else 1 - core) * half + k
        yield 1, [far[0, n * slots + at] for n in range(3)], [held.at[h, n, k] for n in range(3)]


def forward(
    g_idx, u_idx, d_idx, far, core, xa, gw, uw, dw, ra, rb, dgate, dup, hid, held, sems, gate, up, dhid
):
    copies = fetch((ra, rb), held, sems)
    blocks = xa.shape[1] // TILE // 2
    hidden = gate.shape[0] // 2
    for acc in (gate, up, dhid):
        acc[...] = jnp.zeros_like(acc)
    slots = slot_list(core[0], (g_idx, u_idx, d_idx), far, (gw, uw, dw), held, copies)
    for side, (gv, uv, dv), (g_t, u_t, d_t) in slots:
        for v, w, acc in ((gv, g_t, gate), (uv, u_t, up)):
            safe = jnp.maximum(v, 0)
            val = dot(lanes(xa, safe >> 2), w[...], (1, 0))
            acc[side * hidden + (safe & 3)] += jnp.where(v >= 0, val, 0.0)
        safe = jnp.maximum(dv, 0)
        val = dot(lanes(xa, blocks + (safe & 31)), d_t[...], (1, 1))
        dhid[side * hidden + (safe >> 5)] += jnp.where(dv >= 0, val, 0.0)
    for b in range(gate.shape[0]):
        g, u, dh = gate[b], up[b], dhid[b]
        sig = jax.nn.sigmoid(g)
        act = g * sig
        hid[b] = (act * u).astype(BF16)
        dgate[b] = (dh * u * sig * (1.0 + g * (1.0 - sig))).astype(BF16)
        dup[b] = (dh * act).astype(BF16)


def back(g_idx, u_idx, far, core, place, dgate, dup, gw, uw, ra, rb, give, *rest):
    keep, (held, sems, acc) = rest[:-3], rest[-3:]
    copies = fetch((ra, rb), held, sems)
    hidden = dgate.shape[0] // 2
    acc[...] = jnp.zeros_like(acc)
    slots = slot_list(core[0], (g_idx, u_idx, u_idx), far, (gw, uw, uw), held, copies)
    for side, vs, ws in slots:
        for v, w, grad in zip(vs[:2], ws[:2], (dgate, dup)):
            safe = jnp.maximum(v, 0)
            val = dot(grad[side * hidden + (safe & 3)], w[...], (1, 1))
            acc[safe >> 2] += jnp.where(v >= 0, val, 0.0)
    here = keep[0].shape[0]
    me = place[0]
    near = me + 1 - 2 * (me & 1)
    for k in range(len(keep)):
        row = lambda x: pl.ds(pl.multiple_of(((x + 2 * k) & (2 * len(keep) - 1)) * here, here), here)
        for b in range(acc.shape[0]):
            at = slice(b * TILE, (b + 1) * TILE)
            give[k, :, at] = acc[b, row(near), :].astype(BF16)
            keep[k][:, at] = acc[b, row(me), :].astype(BF16)


def tile_terms(
    g_idx, u_idx, d_idx, far, core, xa, dgate, dup, hid, own_mine, own_theirs, far_mine, far_theirs
):
    blocks = xa.shape[1] // TILE // 2
    hidden = dgate.shape[0] // 2
    first = core[0] == 0
    sets = (
        (1, lambda n, s: far[0, n * CAP + s], far_mine, far_theirs),
        (0, lambda n, s: (g_idx, u_idx, d_idx)[n][0, s], own_mine, own_theirs),
    )
    for side, index, mine, theirs in sets:
        for slot in range(CAP):
            outs = []
            for n, grad in ((0, dgate), (1, dup)):
                v = index(n, slot)
                safe = jnp.maximum(v, 0)
                val = dot(lanes(xa, safe >> 2), grad[side * hidden + (safe & 3)], (0, 0))
                outs.append(jnp.where(v >= 0, val, 0.0))
            v = index(2, slot)
            safe = jnp.maximum(v, 0)
            val = dot(hid[side * hidden + (safe >> 5)], lanes(xa, blocks + (safe & 31)), (0, 0))
            outs.append(jnp.where(v >= 0, val, 0.0))
            for k, val in enumerate(outs):
                for half in range(2):
                    even = val[64 * half : 64 * half + 32]
                    odd = val[64 * half + 32 : 64 * half + 64]
                    at = (2 * slot + half, slice(None), slice(k * TILE, (k + 1) * TILE))
                    mine[at] = jnp.where(first, even, odd).astype(BF16)
                    theirs[at] = jnp.where(first, odd, even).astype(BF16)


def beside():
    pairs = []
    for zh in range(4):
        for c in range(2):
            for zl in range(2):
                to = (zh if c == 0 else (zh + (1 if zl else -1)) % 4, c, 1 - zl)
                pairs.append(((zh * 2 + c) * 2 + zl, (to[0] * 2 + to[1]) * 2 + to[2]))
    return pairs


CAP = 16

SMEM = pl.BlockSpec(memory_space=pltpu.SMEM)
VMEM = pl.BlockSpec(memory_space=pltpu.VMEM)
HBM = pl.BlockSpec(memory_space=pltpu.HBM)
SWAP = [(0, 1), (1, 0)]
LAYERS = ("zh", "c", "zl")


def call(kernel, flops, out_shape, scalars, arrays, halves=(), scratch=(), mib=16):
    if halves:
        held = pltpu.VMEM((len(halves), *halves[0].shape), BF16)
        scratch = (held, pltpu.SemaphoreType.DMA((len(halves),)), *scratch)
    return pl.pallas_call(
        kernel,
        out_shape=out_shape,
        in_specs=[SMEM] * len(scalars) + [VMEM] * len(arrays) + [HBM] * len(halves),
        out_specs=(VMEM,) * len(out_shape),
        scratch_shapes=list(scratch),
        compiler_params=pltpu.CompilerParams(vmem_limit_bytes=mib << 20),
        cost_estimate=pl.CostEstimate(flops=flops, bytes_accessed=6 << 20, transcendentals=0),
        name=kernel.__name__,
    )(*scalars, *arrays, *halves)


def per_device(
    tokens, grad_out, gate_tiles, up_tiles, down_tiles, gate_index, up_index, down_index
):
    here, width = tokens.shape
    line = lax.axis_size("x")
    rows, slots = here * line, gate_tiles.shape[1]
    blocks, hidden = width // TILE, 8
    pairs = lax.axis_size(DP) // 2
    gw, uw, dw = gate_tiles[0], up_tiles[0], down_tiles[0]
    at_core = lax.axis_index("c").astype(jnp.int32)
    core = at_core.reshape(1)
    with jax.named_scope("gather"):
        send = pl.pallas_call(
            spread,
            out_shape=jax.ShapeDtypeStruct((line, here, 2 * width), BF16),
            in_specs=[pl.BlockSpec(memory_space=pl.ANY)] * 2,
            out_specs=pl.BlockSpec(memory_space=pl.ANY),
            scratch_shapes=[pltpu.SemaphoreType.DMA((line, 2))],
            name="spread",
        )(tokens, grad_out)
        xa = lax.all_to_all(send, "x", 0, 0, tiled=True).reshape(rows, 2 * width)
    with jax.named_scope("weights"):
        part_of = lambda w: lax.dynamic_slice_in_dim(w, at_core * (slots // 2), slots // 2)
        stack = jnp.stack([part_of(w) for w in (gw, uw, dw)])
        index = jnp.concatenate([gate_index, up_index, down_index], axis=1)
        stack, index = lax.optimization_barrier((stack, index))
        far = lax.ppermute(index, "zl", SWAP)
        ra = lax.ppermute(stack, LAYERS, beside())
        ra, far = lax.optimization_barrier((ra, far))
        rb = lax.ppermute(ra, "c", SWAP)
    own = (gate_index, up_index, down_index)
    work = 2 * rows * TILE * TILE * 2 * slots
    shape = lambda *dims: jax.ShapeDtypeStruct(dims, BF16)
    dgate, dup, hid = call(
        forward,
        3 * work,
        (shape(hidden, rows, TILE),) * 3,
        (*own, far, core),
        (xa, gw, uw, dw),
        (ra, rb),
        [pltpu.VMEM((hidden, rows, TILE), F32)] * 3,
    )
    give, *keep = call(
        back,
        2 * work,
        (shape(line // 2, here, width),) + (shape(here, width),) * (line // 2),
        (*own[:2], far, core, lax.axis_index("x").astype(jnp.int32).reshape(1)),
        (dgate, dup, gw, uw),
        (ra, rb),
        [pltpu.VMEM((blocks, rows, TILE), F32)],
    )
    own_mine, own_theirs, far_mine, far_theirs = call(
        tile_terms,
        3 * work,
        (shape(pairs, 32, 3 * TILE),) * 4,
        (*own, far, core),
        (xa, dgate, dup, hid),
    )
    add = lambda *terms: sum(t.astype(F32) for t in terms).astype(BF16)
    with jax.named_scope("partials"):
        got = lax.ppermute(give, "x", [(i, i ^ 1) for i in range(line)])
    with jax.named_scope("cores"):
        far_got = lax.ppermute(far_theirs, "c", SWAP)
        own_got = lax.ppermute(own_theirs, "c", SWAP)
    with jax.named_scope("layers"):
        near = lax.ppermute(add(far_mine, far_got), LAYERS, beside())
    with jax.named_scope("tile_sums"):
        own_sum, got = lax.optimization_barrier((add(own_mine, own_got), got))
        grads = lax.all_to_all(add(own_sum, near), ("zh", "y"), 0, 0, tiled=True)
        sums = jnp.sum(grads.astype(F32), axis=0)
    with jax.named_scope("partials"):
        pair = [add(keep[k], got[k]) for k in range(line // 2)]
        ring = lambda d: [(i, (i + d) % line) for i in range(line)]
        came = [lax.ppermute(pair[k], "x", ring(2 * k)) for k in (1, 3, 2)]
        input_sum = add(*[t.astype(F32) for t in (keep[0], got[0])], *came)
    return (input_sum, sums[None])


def solution(mesh):
    fine = Mesh(mesh.devices.reshape(4, 8, 2, 2, 8), DP + TEN)
    both = P(DP + TEN, None)
    return jax.shard_map(
        per_device,
        mesh=fine,
        in_specs=(both, both)
        + (P(TEN, None, None, None),) * 3
        + (P(TEN, None),) * 3,
        out_specs=(both, P(TEN, DP, None)),
        check_vma=False,
    )
```

```python
import jax
import jax.numpy as jnp
from jax import lax
from jax.experimental import pallas as pl
from jax.experimental.pallas import tpu as pltpu
from jax.sharding import Mesh, PartitionSpec as P

TILE = 128
DP = ("zh", "y", "c")
TEN = ("zl", "x")
F32 = jnp.float32
BF16 = jnp.bfloat16


def lanes(ref, tile_at):
    return ref[:, pl.ds(pl.multiple_of(tile_at * TILE, TILE), TILE)]


def dot(left, right, on):
    return lax.dot_general(left, right, ((on[:1], on[1:]), ((), ())), preferred_element_type=F32)


def spread(tokens, grad_out, out, sems):
    width = tokens.shape[1]
    copies = [
        pltpu.make_async_copy(t, out.at[n, :, pl.ds(k * width, width)], sems.at[n, k])
        for n in range(out.shape[0])
        for k, t in enumerate((tokens, grad_out))
    ]
    for copy in copies:
        copy.start()
    for copy in copies:
        copy.wait()


def fetch(halves, held, sems):
    copies = [pltpu.make_async_copy(r, held.at[h], sems.at[h]) for h, r in enumerate(halves)]
    for copy in copies:
        copy.start()
    return copies


def slot_list(core, own, far, own_w, held, copies):
    slots = own_w[0].shape[0]
    half = slots // 2
    for s in range(slots):
        yield 0, [i[0, s] for i in own], [w.at[s] for w in own_w]
    for j in range(slots):
        h, k = divmod(j, half)
        if k == 0:
            copies[h].wait()
        at = (core if h == 0 else 1 - core) * half + k
        yield 1, [far[0, n * slots + at] for n in range(3)], [held.at[h, n, k] for n in range(3)]


def forward(
    g_idx, u_idx, d_idx, far, core, xa, gw, uw, dw, ra, rb, dgate, dup, hid, held, sems, gate, up, dhid
):
    copies = fetch((ra, rb), held, sems)
    blocks = xa.shape[1] // TILE // 2
    hidden = gate.shape[0] // 2
    for acc in (gate, up, dhid):
        acc[...] = jnp.zeros_like(acc)
    slots = slot_list(core[0], (g_idx, u_idx, d_idx), far, (gw, uw, dw), held, copies)
    for side, (gv, uv, dv), (g_t, u_t, d_t) in slots:
        for v, w, acc in ((gv, g_t, gate), (uv, u_t, up)):
            safe = jnp.maximum(v, 0)
            val = dot(lanes(xa, safe >> 2), w[...], (1, 0))
            acc[side * hidden + (safe & 3)] += jnp.where(v >= 0, val, 0.0)
        safe = jnp.maximum(dv, 0)
        val = dot(lanes(xa, blocks + (safe & 31)), d_t[...], (1, 1))
        dhid[side * hidden + (safe >> 5)] += jnp.where(dv >= 0, val, 0.0)
    for b in range(gate.shape[0]):
        g, u, dh = gate[b], up[b], dhid[b]
        sig = jax.nn.sigmoid(g)
        act = g * sig
        hid[b] = (act * u).astype(BF16)
        dgate[b] = (dh * u * sig * (1.0 + g * (1.0 - sig))).astype(BF16)
        dup[b] = (dh * act).astype(BF16)


def back(g_idx, u_idx, far, core, place, dgate, dup, gw, uw, ra, rb, give, *rest):
    keep, (held, sems, acc) = rest[:-3], rest[-3:]
    copies = fetch((ra, rb), held, sems)
    hidden = dgate.shape[0] // 2
    acc[...] = jnp.zeros_like(acc)
    slots = slot_list(core[0], (g_idx, u_idx, u_idx), far, (gw, uw, uw), held, copies)
    for side, vs, ws in slots:
        for v, w, grad in zip(vs[:2], ws[:2], (dgate, dup)):
            safe = jnp.maximum(v, 0)
            val = dot(grad[side * hidden + (safe & 3)], w[...], (1, 1))
            acc[safe >> 2] += jnp.where(v >= 0, val, 0.0)
    here = keep[0].shape[0]
    me = place[0]
    near = me + 1 - 2 * (me & 1)
    for k in range(len(keep)):
        row = lambda x: pl.ds(pl.multiple_of(((x + 2 * k) & (2 * len(keep) - 1)) * here, here), here)
        for b in range(acc.shape[0]):
            at = slice(b * TILE, (b + 1) * TILE)
            give[k, :, at] = acc[b, row(near), :].astype(BF16)
            keep[k][:, at] = acc[b, row(me), :].astype(BF16)


def tile_terms(
    g_idx, u_idx, d_idx, far, core, xa, dgate, dup, hid, own_mine, own_theirs, far_mine, far_theirs
):
    blocks = xa.shape[1] // TILE // 2
    hidden = dgate.shape[0] // 2
    first = core[0] == 0
    sets = (
        (1, lambda n, s: far[0, n * CAP + s], far_mine, far_theirs),
        (0, lambda n, s: (g_idx, u_idx, d_idx)[n][0, s], own_mine, own_theirs),
    )
    for side, index, mine, theirs in sets:
        for slot in range(CAP):
            outs = []
            for n, grad in ((0, dgate), (1, dup)):
                v = index(n, slot)
                safe = jnp.maximum(v, 0)
                val = dot(lanes(xa, safe >> 2), grad[side * hidden + (safe & 3)], (0, 0))
                outs.append(jnp.where(v >= 0, val, 0.0))
            v = index(2, slot)
            safe = jnp.maximum(v, 0)
            val = dot(hid[side * hidden + (safe >> 5)], lanes(xa, blocks + (safe & 31)), (0, 0))
            outs.append(jnp.where(v >= 0, val, 0.0))
            for k, val in enumerate(outs):
                for half in range(2):
                    even = val[64 * half : 64 * half + 32]
                    odd = val[64 * half + 32 : 64 * half + 64]
                    at = (2 * slot + half, slice(None), slice(k * TILE, (k + 1) * TILE))
                    mine[at] = jnp.where(first, even, odd).astype(BF16)
                    theirs[at] = jnp.where(first, odd, even).astype(BF16)


def total(left, right, out):
    out[...] = (left[...].astype(F32) + right[...].astype(F32)).astype(BF16)


def beside():
    pairs = []
    for zh in range(4):
        for c in range(2):
            for zl in range(2):
                to = (zh if c == 0 else (zh + (1 if zl else -1)) % 4, c, 1 - zl)
                pairs.append(((zh * 2 + c) * 2 + zl, (to[0] * 2 + to[1]) * 2 + to[2]))
    return pairs


CAP = 16

SMEM = pl.BlockSpec(memory_space=pltpu.SMEM)
VMEM = pl.BlockSpec(memory_space=pltpu.VMEM)
HBM = pl.BlockSpec(memory_space=pltpu.HBM)
SWAP = [(0, 1), (1, 0)]
LAYERS = ("zh", "c", "zl")


def call(kernel, flops, out_shape, scalars, arrays, halves=(), scratch=(), mib=16):
    if halves:
        held = pltpu.VMEM((len(halves), *halves[0].shape), BF16)
        scratch = (held, pltpu.SemaphoreType.DMA((len(halves),)), *scratch)
    return pl.pallas_call(
        kernel,
        out_shape=out_shape,
        in_specs=[SMEM] * len(scalars) + [VMEM] * len(arrays) + [HBM] * len(halves),
        out_specs=(VMEM,) * len(out_shape),
        scratch_shapes=list(scratch),
        compiler_params=pltpu.CompilerParams(vmem_limit_bytes=mib << 20),
        cost_estimate=pl.CostEstimate(flops=flops, bytes_accessed=6 << 20, transcendentals=0),
        name=kernel.__name__,
    )(*scalars, *arrays, *halves)


def per_device(
    tokens, grad_out, gate_tiles, up_tiles, down_tiles, gate_index, up_index, down_index
):
    here, width = tokens.shape
    line = lax.axis_size("x")
    rows, slots = here * line, gate_tiles.shape[1]
    blocks, hidden = width // TILE, 8
    pairs = lax.axis_size(DP) // 2
    gw, uw, dw = gate_tiles[0], up_tiles[0], down_tiles[0]
    at_core = lax.axis_index("c").astype(jnp.int32)
    core = at_core.reshape(1)
    with jax.named_scope("gather"):
        send = pl.pallas_call(
            spread,
            out_shape=jax.ShapeDtypeStruct((line, here, 2 * width), BF16),
            in_specs=[VMEM] * 2,
            out_specs=pl.BlockSpec(memory_space=pl.ANY),
            scratch_shapes=[pltpu.SemaphoreType.DMA((line, 2))],
            name="spread",
        )(tokens, grad_out)
        xa = lax.all_to_all(send, "x", 0, 0, tiled=True).reshape(rows, 2 * width)
    with jax.named_scope("weights"):
        part_of = lambda w: lax.dynamic_slice_in_dim(w, at_core * (slots // 2), slots // 2)
        stack = jnp.stack([part_of(w) for w in (gw, uw, dw)])
        index = jnp.concatenate([gate_index, up_index, down_index], axis=1)
        stack, index = lax.optimization_barrier((stack, index))
        far = lax.ppermute(index, "zl", SWAP)
        ra = lax.ppermute(stack, LAYERS, beside())
        ra, far = lax.optimization_barrier((ra, far))
        rb = lax.ppermute(ra, "c", SWAP)
    own = (gate_index, up_index, down_index)
    work = 2 * rows * TILE * TILE * 2 * slots
    shape = lambda *dims: jax.ShapeDtypeStruct(dims, BF16)
    dgate, dup, hid = call(
        forward,
        3 * work,
        (shape(hidden, rows, TILE),) * 3,
        (*own, far, core),
        (xa, gw, uw, dw),
        (ra, rb),
        [pltpu.VMEM((hidden, rows, TILE), F32)] * 3,
    )
    give, *keep = call(
        back,
        2 * work,
        (shape(line // 2, here, width),) + (shape(here, width),) * (line // 2),
        (*own[:2], far, core, lax.axis_index("x").astype(jnp.int32).reshape(1)),
        (dgate, dup, gw, uw),
        (ra, rb),
        [pltpu.VMEM((blocks, rows, TILE), F32)],
    )
    own_mine, own_theirs, far_mine, far_theirs = call(
        tile_terms,
        3 * work,
        (shape(pairs, 32, 3 * TILE),) * 4,
        (*own, far, core),
        (xa, dgate, dup, hid),
    )
    add = lambda *terms: sum(t.astype(F32) for t in terms).astype(BF16)
    with jax.named_scope("partials"):
        got = lax.ppermute(give, "x", [(i, i ^ 1) for i in range(line)])
    with jax.named_scope("cores"):
        far_got = lax.ppermute(far_theirs, "c", SWAP)
        own_got = lax.ppermute(own_theirs, "c", SWAP)
    with jax.named_scope("layers"):
        near = lax.ppermute(add(far_mine, far_got), LAYERS, beside())
    with jax.named_scope("tile_sums"):
        own_sum, got = lax.optimization_barrier((add(own_mine, own_got), got))
        block = pl.BlockSpec((8, 32, 3 * TILE), lambda i: (i, 0, 0))
        set_sum = pl.pallas_call(
            total,
            grid=(pairs // 8,),
            out_shape=shape(pairs, 32, 3 * TILE),
            in_specs=[block] * 2,
            out_specs=block,
            compiler_params=pltpu.CompilerParams(vmem_limit_bytes=8 << 20),
            name="total",
        )(own_sum, near)
        grads = lax.all_to_all(set_sum, ("zh", "y"), 0, 0, tiled=True)
        sums = jnp.sum(grads.astype(F32), axis=0)
    with jax.named_scope("partials"):
        pair = [add(keep[k], got[k]) for k in range(line // 2)]
        ring = lambda d: [(i, (i + d) % line) for i in range(line)]
        came = [lax.ppermute(pair[k], "x", ring(2 * k)) for k in (1, 3, 2)]
        input_sum = add(*[t.astype(F32) for t in (keep[0], got[0])], *came)
    return (input_sum, sums[None])


def solution(mesh):
    fine = Mesh(mesh.devices.reshape(4, 8, 2, 2, 8), DP + TEN)
    both = P(DP + TEN, None)
    return jax.shard_map(
        per_device,
        mesh=fine,
        in_specs=(both, both)
        + (P(TEN, None, None, None),) * 3
        + (P(TEN, None),) * 3,
        out_specs=(both, P(TEN, DP, None)),
        check_vma=False,
    )
```

```python
import jax
import jax.numpy as jnp
from jax import lax
from jax.experimental import pallas as pl
from jax.experimental.pallas import tpu as pltpu
from jax.sharding import Mesh, PartitionSpec as P

TILE = 128
DP = ("zh", "y", "c")
TEN = ("zl", "x")
F32 = jnp.float32
BF16 = jnp.bfloat16


def lanes(ref, tile_at):
    return ref[:, pl.ds(pl.multiple_of(tile_at * TILE, TILE), TILE)]


def dot(left, right, on):
    return lax.dot_general(left, right, ((on[:1], on[1:]), ((), ())), preferred_element_type=F32)


def fetch(halves, held, sems):
    copies = [pltpu.make_async_copy(r, held.at[h], sems.at[h]) for h, r in enumerate(halves)]
    for copy in copies:
        copy.start()
    return copies


def slot_list(core, own, far, own_w, held, copies):
    slots = own_w[0].shape[0]
    half = slots // 2
    for s in range(slots):
        yield 0, [i[0, s] for i in own], [w.at[s] for w in own_w]
    for j in range(slots):
        h, k = divmod(j, half)
        if k == 0:
            copies[h].wait()
        at = (core if h == 0 else 1 - core) * half + k
        yield 1, [far[0, n * slots + at] for n in range(3)], [held.at[h, n, k] for n in range(3)]


def forward(
    g_idx, u_idx, d_idx, far, core, xa, gw, uw, dw, ra, rb, dgate, dup, hid, held, sems, gate, up, dhid
):
    copies = fetch((ra, rb), held, sems)
    blocks = xa.shape[1] // TILE // 2
    hidden = gate.shape[0] // 2
    for acc in (gate, up, dhid):
        acc[...] = jnp.zeros_like(acc)
    slots = slot_list(core[0], (g_idx, u_idx, d_idx), far, (gw, uw, dw), held, copies)
    for side, (gv, uv, dv), (g_t, u_t, d_t) in slots:
        for v, w, acc in ((gv, g_t, gate), (uv, u_t, up)):
            safe = jnp.maximum(v, 0)
            val = dot(lanes(xa, safe >> 2), w[...], (1, 0))
            acc[side * hidden + (safe & 3)] += jnp.where(v >= 0, val, 0.0)
        safe = jnp.maximum(dv, 0)
        val = dot(lanes(xa, blocks + (safe & 31)), d_t[...], (1, 1))
        dhid[side * hidden + (safe >> 5)] += jnp.where(dv >= 0, val, 0.0)
    for b in range(gate.shape[0]):
        g, u, dh = gate[b], up[b], dhid[b]
        sig = jax.nn.sigmoid(g)
        act = g * sig
        hid[b] = (act * u).astype(BF16)
        dgate[b] = (dh * u * sig * (1.0 + g * (1.0 - sig))).astype(BF16)
        dup[b] = (dh * act).astype(BF16)


def back(g_idx, u_idx, far, core, place, dgate, dup, gw, uw, ra, rb, give, *rest):
    keep, (held, sems, acc) = rest[:-3], rest[-3:]
    copies = fetch((ra, rb), held, sems)
    hidden = dgate.shape[0] // 2
    acc[...] = jnp.zeros_like(acc)
    slots = slot_list(core[0], (g_idx, u_idx, u_idx), far, (gw, uw, uw), held, copies)
    for side, vs, ws in slots:
        for v, w, grad in zip(vs[:2], ws[:2], (dgate, dup)):
            safe = jnp.maximum(v, 0)
            val = dot(grad[side * hidden + (safe & 3)], w[...], (1, 1))
            acc[safe >> 2] += jnp.where(v >= 0, val, 0.0)
    here = keep[0].shape[0]
    me = place[0]
    near = me + 1 - 2 * (me & 1)
    for k in range(len(keep)):
        row = lambda x: pl.ds(pl.multiple_of(((x + 2 * k) & (2 * len(keep) - 1)) * here, here), here)
        for b in range(acc.shape[0]):
            at = slice(b * TILE, (b + 1) * TILE)
            give[k, :, at] = acc[b, row(near), :].astype(BF16)
            keep[k][:, at] = acc[b, row(me), :].astype(BF16)


def tile_terms(
    g_idx, u_idx, d_idx, far, core, xa, dgate, dup, hid, own_mine, own_theirs, far_mine, far_theirs
):
    blocks = xa.shape[1] // TILE // 2
    hidden = dgate.shape[0] // 2
    first = core[0] == 0
    sets = (
        (1, lambda n, s: far[0, n * CAP + s], far_mine, far_theirs),
        (0, lambda n, s: (g_idx, u_idx, d_idx)[n][0, s], own_mine, own_theirs),
    )
    for side, index, mine, theirs in sets:
        for slot in range(CAP):
            outs = []
            for n, grad in ((0, dgate), (1, dup)):
                v = index(n, slot)
                safe = jnp.maximum(v, 0)
                val = dot(lanes(xa, safe >> 2), grad[side * hidden + (safe & 3)], (0, 0))
                outs.append(jnp.where(v >= 0, val, 0.0))
            v = index(2, slot)
            safe = jnp.maximum(v, 0)
            val = dot(hid[side * hidden + (safe >> 5)], lanes(xa, blocks + (safe & 31)), (0, 0))
            outs.append(jnp.where(v >= 0, val, 0.0))
            for k, val in enumerate(outs):
                for half in range(2):
                    even = val[64 * half : 64 * half + 32]
                    odd = val[64 * half + 32 : 64 * half + 64]
                    at = (2 * slot + half, slice(None), slice(k * TILE, (k + 1) * TILE))
                    mine[at] = jnp.where(first, even, odd).astype(BF16)
                    theirs[at] = jnp.where(first, odd, even).astype(BF16)


def settle(far, out):
    out[...] = jnp.maximum(far[...], -1)


def beside():
    pairs = []
    for zh in range(4):
        for c in range(2):
            for zl in range(2):
                to = (zh if c == 0 else (zh + (1 if zl else -1)) % 4, c, 1 - zl)
                pairs.append(((zh * 2 + c) * 2 + zl, (to[0] * 2 + to[1]) * 2 + to[2]))
    return pairs


CAP = 16

SMEM = pl.BlockSpec(memory_space=pltpu.SMEM)
VMEM = pl.BlockSpec(memory_space=pltpu.VMEM)
HBM = pl.BlockSpec(memory_space=pltpu.HBM)
SWAP = [(0, 1), (1, 0)]
LAYERS = ("zh", "c", "zl")


def call(kernel, flops, out_shape, scalars, arrays, halves=(), scratch=(), mib=16):
    if halves:
        held = pltpu.VMEM((len(halves), *halves[0].shape), BF16)
        scratch = (held, pltpu.SemaphoreType.DMA((len(halves),)), *scratch)
    return pl.pallas_call(
        kernel,
        out_shape=out_shape,
        in_specs=[SMEM] * len(scalars) + [VMEM] * len(arrays) + [HBM] * len(halves),
        out_specs=(VMEM,) * len(out_shape),
        scratch_shapes=list(scratch),
        compiler_params=pltpu.CompilerParams(vmem_limit_bytes=mib << 20),
        cost_estimate=pl.CostEstimate(flops=flops, bytes_accessed=6 << 20, transcendentals=0),
        name=kernel.__name__,
    )(*scalars, *arrays, *halves)


def per_device(
    tokens, grad_out, gate_tiles, up_tiles, down_tiles, gate_index, up_index, down_index
):
    here, width = tokens.shape
    line = lax.axis_size("x")
    rows, slots = here * line, gate_tiles.shape[1]
    blocks, hidden = width // TILE, 8
    pairs = lax.axis_size(DP) // 2
    gw, uw, dw = gate_tiles[0], up_tiles[0], down_tiles[0]
    at_core = lax.axis_index("c").astype(jnp.int32)
    core = at_core.reshape(1)
    with jax.named_scope("gather"):
        both = jnp.concatenate([tokens, grad_out], axis=1)
        send = jnp.broadcast_to(both[None], (line, here, 2 * width))
        xa = lax.all_to_all(send, "x", 0, 0, tiled=True).reshape(rows, 2 * width)
    with jax.named_scope("weights"):
        part_of = lambda w: lax.dynamic_slice_in_dim(w, at_core * (slots // 2), slots // 2)
        stack = jnp.stack([part_of(w) for w in (gw, uw, dw)])
        index = jnp.concatenate([gate_index, up_index, down_index], axis=1)
        stack, index = lax.optimization_barrier((stack, index))
        far = lax.ppermute(index, "zl", SWAP)
        ra = lax.ppermute(stack, LAYERS, beside())
        ra, far = lax.optimization_barrier((ra, far))
        far = pl.pallas_call(
            settle,
            out_shape=jax.ShapeDtypeStruct(far.shape, far.dtype),
            in_specs=[VMEM],
            out_specs=VMEM,
            compiler_params=pltpu.CompilerParams(vmem_limit_bytes=1 << 20),
            cost_estimate=pl.CostEstimate(flops=10 ** 10, bytes_accessed=0, transcendentals=0),
            name="settle",
        )(far)
        ra, far = lax.optimization_barrier((ra, far))
        rb = lax.ppermute(ra, "c", SWAP)
    own = (gate_index, up_index, down_index)
    work = 2 * rows * TILE * TILE * 2 * slots
    shape = lambda *dims: jax.ShapeDtypeStruct(dims, BF16)
    dgate, dup, hid = call(
        forward,
        3 * work,
        (shape(hidden, rows, TILE),) * 3,
        (*own, far, core),
        (xa, gw, uw, dw),
        (ra, rb),
        [pltpu.VMEM((hidden, rows, TILE), F32)] * 3,
    )
    give, *keep = call(
        back,
        2 * work,
        (shape(line // 2, here, width),) + (shape(here, width),) * (line // 2),
        (*own[:2], far, core, lax.axis_index("x").astype(jnp.int32).reshape(1)),
        (dgate, dup, gw, uw),
        (ra, rb),
        [pltpu.VMEM((blocks, rows, TILE), F32)],
    )
    own_mine, own_theirs, far_mine, far_theirs = call(
        tile_terms,
        3 * work,
        (shape(pairs, 32, 3 * TILE),) * 4,
        (*own, far, core),
        (xa, dgate, dup, hid),
    )
    add = lambda *terms: sum(t.astype(F32) for t in terms).astype(BF16)
    with jax.named_scope("partials"):
        got = lax.ppermute(give, "x", [(i, i ^ 1) for i in range(line)])
    with jax.named_scope("cores"):
        far_got = lax.ppermute(far_theirs, "c", SWAP)
        own_got = lax.ppermute(own_theirs, "c", SWAP)
    with jax.named_scope("layers"):
        near = lax.ppermute(add(far_mine, far_got), LAYERS, beside())
    with jax.named_scope("tile_sums"):
        own_sum, got = lax.optimization_barrier((add(own_mine, own_got), got))
        grads = lax.all_to_all(add(own_sum, near), ("zh", "y"), 0, 0, tiled=True)
        sums = jnp.sum(grads.astype(F32), axis=0)
    with jax.named_scope("partials"):
        pair = [add(keep[k], got[k]) for k in range(line // 2)]
        ring = lambda d: [(i, (i + d) % line) for i in range(line)]
        came = [lax.ppermute(pair[k], "x", ring(2 * k)) for k in (1, 3, 2)]
        input_sum = add(*[t.astype(F32) for t in (keep[0], got[0])], *came)
    return (input_sum, sums[None])


def solution(mesh):
    fine = Mesh(mesh.devices.reshape(4, 8, 2, 2, 8), DP + TEN)
    both = P(DP + TEN, None)
    return jax.shard_map(
        per_device,
        mesh=fine,
        in_specs=(both, both)
        + (P(TEN, None, None, None),) * 3
        + (P(TEN, None),) * 3,
        out_specs=(both, P(TEN, DP, None)),
        check_vma=False,
    )
```

```python
import jax
import jax.numpy as jnp
from jax import lax
from jax.experimental import pallas as pl
from jax.experimental.pallas import tpu as pltpu
from jax.sharding import Mesh, PartitionSpec as P

TILE = 128
DP = ("zh", "y", "c")
TEN = ("zl", "x")
F32 = jnp.float32
BF16 = jnp.bfloat16


def lanes(ref, tile_at):
    return ref[:, pl.ds(pl.multiple_of(tile_at * TILE, TILE), TILE)]


def dot(left, right, on):
    return lax.dot_general(left, right, ((on[:1], on[1:]), ((), ())), preferred_element_type=F32)


def fetch(halves, held, sems):
    copies = [pltpu.make_async_copy(r, held.at[h], sems.at[h]) for h, r in enumerate(halves)]
    for copy in copies:
        copy.start()
    return copies


def slot_list(core, own, far, own_w, held, copies):
    slots = own_w[0].shape[0]
    half = slots // 2
    for s in range(slots):
        yield 0, [i[0, s] for i in own], [w.at[s] for w in own_w]
    for j in range(slots):
        h, k = divmod(j, half)
        if k == 0:
            copies[h].wait()
        at = (core if h == 0 else 1 - core) * half + k
        yield 1, [far[0, n * slots + at] for n in range(3)], [held.at[h, n, k] for n in range(3)]


def forward(
    g_idx, u_idx, d_idx, far, core, xa, gw, uw, dw, ra, rb, dgate, dup, hid, held, sems, gate, up, dhid
):
    copies = fetch((ra, rb), held, sems)
    blocks = xa.shape[1] // TILE // 2
    hidden = gate.shape[0] // 2
    for acc in (gate, up, dhid):
        acc[...] = jnp.zeros_like(acc)
    slots = slot_list(core[0], (g_idx, u_idx, d_idx), far, (gw, uw, dw), held, copies)
    for side, (gv, uv, dv), (g_t, u_t, d_t) in slots:
        for v, w, acc in ((gv, g_t, gate), (uv, u_t, up)):
            safe = jnp.maximum(v, 0)
            val = dot(lanes(xa, safe >> 2), w[...], (1, 0))
            acc[side * hidden + (safe & 3)] += jnp.where(v >= 0, val, 0.0)
        safe = jnp.maximum(dv, 0)
        val = dot(lanes(xa, blocks + (safe & 31)), d_t[...], (1, 1))
        dhid[side * hidden + (safe >> 5)] += jnp.where(dv >= 0, val, 0.0)
    for b in range(gate.shape[0]):
        g, u, dh = gate[b], up[b], dhid[b]
        sig = jax.nn.sigmoid(g)
        act = g * sig
        hid[b] = (act * u).astype(BF16)
        dgate[b] = (dh * u * sig * (1.0 + g * (1.0 - sig))).astype(BF16)
        dup[b] = (dh * act).astype(BF16)


def back(g_idx, u_idx, far, core, place, dgate, dup, gw, uw, ra, rb, give, *rest):
    keep, (held, sems, acc) = rest[:-3], rest[-3:]
    copies = fetch((ra, rb), held, sems)
    hidden = dgate.shape[0] // 2
    acc[...] = jnp.zeros_like(acc)
    slots = slot_list(core[0], (g_idx, u_idx, u_idx), far, (gw, uw, uw), held, copies)
    for side, vs, ws in slots:
        for v, w, grad in zip(vs[:2], ws[:2], (dgate, dup)):
            safe = jnp.maximum(v, 0)
            val = dot(grad[side * hidden + (safe & 3)], w[...], (1, 1))
            acc[safe >> 2] += jnp.where(v >= 0, val, 0.0)
    here = keep[0].shape[0]
    me = place[0]
    near = me + 1 - 2 * (me & 1)
    for k in range(len(keep)):
        row = lambda x: pl.ds(pl.multiple_of(((x + 2 * k) & (2 * len(keep) - 1)) * here, here), here)
        for b in range(acc.shape[0]):
            at = slice(b * TILE, (b + 1) * TILE)
            give[k, :, at] = acc[b, row(near), :].astype(BF16)
            keep[k][:, at] = acc[b, row(me), :].astype(BF16)


def tile_terms(
    g_idx, u_idx, d_idx, far, core, xa, dgate, dup, hid, own_mine, own_theirs, far_mine, far_theirs
):
    blocks = xa.shape[1] // TILE // 2
    hidden = dgate.shape[0] // 2
    first = core[0] == 0
    sets = (
        (1, lambda n, s: far[0, n * CAP + s], far_mine, far_theirs),
        (0, lambda n, s: (g_idx, u_idx, d_idx)[n][0, s], own_mine, own_theirs),
    )
    for side, index, mine, theirs in sets:
        for slot in range(CAP):
            outs = []
            for n, grad in ((0, dgate), (1, dup)):
                v = index(n, slot)
                safe = jnp.maximum(v, 0)
                val = dot(lanes(xa, safe >> 2), grad[side * hidden + (safe & 3)], (0, 0))
                outs.append(jnp.where(v >= 0, val, 0.0))
            v = index(2, slot)
            safe = jnp.maximum(v, 0)
            val = dot(hid[side * hidden + (safe >> 5)], lanes(xa, blocks + (safe & 31)), (0, 0))
            outs.append(jnp.where(v >= 0, val, 0.0))
            for k, val in enumerate(outs):
                for half in range(2):
                    even = val[64 * half : 64 * half + 32]
                    odd = val[64 * half + 32 : 64 * half + 64]
                    at = (2 * slot + half, slice(None), slice(k * TILE, (k + 1) * TILE))
                    mine[at] = jnp.where(first, even, odd).astype(BF16)
                    theirs[at] = jnp.where(first, odd, even).astype(BF16)


def beside():
    pairs = []
    for zh in range(4):
        for c in range(2):
            for zl in range(2):
                to = (zh if c == 0 else (zh + (1 if zl else -1)) % 4, c, 1 - zl)
                pairs.append(((zh * 2 + c) * 2 + zl, (to[0] * 2 + to[1]) * 2 + to[2]))
    return pairs


CAP = 16

SMEM = pl.BlockSpec(memory_space=pltpu.SMEM)
VMEM = pl.BlockSpec(memory_space=pltpu.VMEM)
HBM = pl.BlockSpec(memory_space=pltpu.HBM)
SWAP = [(0, 1), (1, 0)]
LAYERS = ("zh", "c", "zl")


def call(kernel, flops, out_shape, scalars, arrays, halves=(), scratch=(), mib=16):
    if halves:
        held = pltpu.VMEM((len(halves), *halves[0].shape), BF16)
        scratch = (held, pltpu.SemaphoreType.DMA((len(halves),)), *scratch)
    return pl.pallas_call(
        kernel,
        out_shape=out_shape,
        in_specs=[SMEM] * len(scalars) + [VMEM] * len(arrays) + [HBM] * len(halves),
        out_specs=(VMEM,) * len(out_shape),
        scratch_shapes=list(scratch),
        compiler_params=pltpu.CompilerParams(vmem_limit_bytes=mib << 20),
        cost_estimate=pl.CostEstimate(flops=flops, bytes_accessed=6 << 20, transcendentals=0),
        name=kernel.__name__,
    )(*scalars, *arrays, *halves)


def per_device(
    tokens, grad_out, gate_tiles, up_tiles, down_tiles, gate_index, up_index, down_index
):
    here, width = tokens.shape
    line = lax.axis_size("x")
    rows, slots = here * line, gate_tiles.shape[1]
    blocks, hidden = width // TILE, 8
    pairs = lax.axis_size(DP) // 2
    gw, uw, dw = gate_tiles[0], up_tiles[0], down_tiles[0]
    at_core = lax.axis_index("c").astype(jnp.int32)
    core = at_core.reshape(1)
    with jax.named_scope("gather"):
        both = jnp.concatenate([tokens, grad_out], axis=1)
        send = jnp.broadcast_to(both[None], (line, here, 2 * width))
        xa = lax.all_to_all(send, "x", 0, 0, tiled=True).reshape(rows, 2 * width)
    with jax.named_scope("weights"):
        part_of = lambda w: lax.dynamic_slice_in_dim(w, at_core * (slots // 2), slots // 2)
        stack = jnp.stack([part_of(w) for w in (gw, uw, dw)])
        index = jnp.concatenate([gate_index, up_index, down_index], axis=1)
        stack, index = lax.optimization_barrier((stack, index))
        far = lax.ppermute(index, "zl", SWAP)
        ra = lax.ppermute(stack, LAYERS, beside())
        ra, far = lax.optimization_barrier((ra, far))
        rb = lax.ppermute(ra, "c", SWAP)
    own = (gate_index, up_index, down_index)
    work = 2 * rows * TILE * TILE * 2 * slots
    shape = lambda *dims: jax.ShapeDtypeStruct(dims, BF16)
    dgate, dup, hid = call(
        forward,
        3 * work,
        (shape(hidden, rows, TILE),) * 3,
        (*own, far, core),
        (xa, gw, uw, dw),
        (ra, rb),
        [pltpu.VMEM((hidden, rows, TILE), F32)] * 3,
    )
    give, *keep = call(
        back,
        2 * work,
        (shape(line // 2, here, width),) + (shape(here, width),) * (line // 2),
        (*own[:2], far, core, lax.axis_index("x").astype(jnp.int32).reshape(1)),
        (dgate, dup, gw, uw),
        (ra, rb),
        [pltpu.VMEM((blocks, rows, TILE), F32)],
    )
    own_mine, own_theirs, far_mine, far_theirs = call(
        tile_terms,
        3 * work,
        (shape(pairs, 32, 3 * TILE),) * 4,
        (*own, far, core),
        (xa, dgate, dup, hid),
    )
    add = lambda *terms: sum(t.astype(F32) for t in terms).astype(BF16)
    with jax.named_scope("partials"):
        got = lax.ppermute(give, "x", [(i, i ^ 1) for i in range(line)])
    with jax.named_scope("cores"):
        far_got = lax.ppermute(far_theirs, "c", SWAP)
        own_got = lax.ppermute(own_theirs, "c", SWAP)
    with jax.named_scope("layers"):
        near = lax.ppermute(add(far_mine, far_got), LAYERS, beside())
    with jax.named_scope("tile_sums"):
        own_sum, give = lax.optimization_barrier((add(own_mine, own_got), give))
        grads = lax.all_to_all(add(own_sum, near), ("zh", "y"), 0, 0, tiled=True)
        sums = jnp.sum(grads.astype(F32), axis=0)
    with jax.named_scope("partials"):
        pair = [add(keep[k], got[k]) for k in range(line // 2)]
        ring = lambda d: [(i, (i + d) % line) for i in range(line)]
        came = [lax.ppermute(pair[k], "x", ring(2 * k)) for k in (1, 3, 2)]
        input_sum = add(*[t.astype(F32) for t in (keep[0], got[0])], *came)
    return (input_sum, sums[None])


def solution(mesh):
    fine = Mesh(mesh.devices.reshape(4, 8, 2, 2, 8), DP + TEN)
    both = P(DP + TEN, None)
    return jax.shard_map(
        per_device,
        mesh=fine,
        in_specs=(both, both)
        + (P(TEN, None, None, None),) * 3
        + (P(TEN, None),) * 3,
        out_specs=(both, P(TEN, DP, None)),
        check_vma=False,
    )
```
